32 devices in a mesh: outer: 2 (over x), lat: 4 (over y, core), lon: 4 (over z).
Axes of the slice: x: 2, y: 2, z: 4, core: 2. Of those that a mesh axis runs over, the one named last changes fastest.
Arguments:
- tokens: bfloat16 [48, 2, 48, 2048], P(('outer', 'lat'), None, 'lon'), may hold values from -6 to 6
- norm_gain: float32 [2048], replicated, may hold values from 0.4 to 1.6
- w_qkv: bfloat16 [2048, 3, 2048], P(None, None, 'outer'), may hold values from -20 to 20
- w_out: bfloat16 [2048, 2048], P('outer'), may hold values from -0.125 to 0.125
- grad_out: bfloat16 [48, 2, 48, 2048], P(('outer', 'lat'), None, 'lon'), may hold values from -6 to 6
Outputs:
- output: bfloat16 [48, 2, 48, 2048], P(('outer', 'lat'), None, 'lon')
- grad_tokens: bfloat16 [48, 2, 48, 2048], P(('outer', 'lat'), None, 'lon')
- grad_wqkv: float32 [2048, 3, 2048], P(None, None, 'outer')
- grad_wout: float32 [2048, 2048], P('outer')
- grad_gain: float32 [2048], replicated
The draws below stay inside these ranges and needn't reach their ends.
All inputs are finite; a program needn't handle non-finite values.
Results may differ from the reference program's by a relative error of at most 0.023.
Values may be sent and summed in bfloat16 or wider, within the bound.
A program may use at most 128 MiB of HBM per device.

```python
import jax
import jax.numpy as jnp
from jax import lax

D = 2048
HEADS = 32
HEAD = 64
LEV = 2
CLAT = 3
WLON = 12
LAT = 48
LON = 48
N_OUTER = 2


def draw_w_qkv(key, part):
    key = jax.random.fold_in(key, 7)
    base = jnp.clip(jax.random.normal(key, (D, 3, D), jnp.float32), -4.0, 4.0) * D ** (-0.5)
    return base.astype(jnp.bfloat16)


def shard_levels(rng, shape, cuts, smallest, largest):
    def one(axis_at, blocks):
        heights = jax.random.uniform(jax.random.fold_in(jax.random.fold_in(rng, 6), axis_at), (blocks,), jnp.float32, smallest / len(cuts), largest / len(cuts))
        return jnp.repeat(jnp.exp(heights), shape[axis_at] // blocks).reshape((-1,) + (1,) * (len(shape) - axis_at - 1))

    loudness = one(*cuts[0])
    for cut in cuts[1:]:
        loudness = loudness * one(*cut)
    return loudness


def centred(rng, shape, scale, limit, shards=(), kind=jnp.bfloat16):
    result = scale * jax.random.normal(rng, shape, jnp.float32)
    if shards:
        result = result * shard_levels(rng, shape, shards, -0.22, 0.18)
    return jnp.clip(result, -limit, limit).astype(kind)


def setup_inputs(seed: int = 0) -> dict:
    arg_keys = jax.random.split(jax.random.key(seed), 6)
    return {
        "tokens": centred(arg_keys[0], (LAT, LEV, LON, D), 1.0, 6.0, ((0, 8), (2, 4))),
        "norm_gain": jnp.clip(1.0 + 0.12 * jax.random.normal(arg_keys[1], (D,), jnp.float32), 0.4, 1.6),
        "w_qkv": draw_w_qkv(jax.random.fold_in(arg_keys[5], 71), 0),
        "w_out": centred(arg_keys[3], (D, D), D ** -0.5, 0.125, ((0, 2),)),
        "grad_out": centred(arg_keys[4], (LAT, LEV, LON, D), 1.0, 6.0, ((0, 8), (2, 4))),
    }


epsilon = 1e-05

def normalize(tokens):
    values_f = tokens.astype(jnp.float32)
    average = lax.optimization_barrier(jnp.mean(values_f, -1, keepdims=True))
    centered = values_f - average
    inverse_std = lax.rsqrt(lax.optimization_barrier(jnp.mean(centered * centered, -1, keepdims=True)) + epsilon)
    return (centered * inverse_std, inverse_std)

def to_windows(tensor):
    latitude, levels, longitude, channels = tensor.shape
    shaped = tensor.reshape(latitude // (2 * CLAT), 2 * CLAT, levels, longitude // WLON, WLON, channels)
    shaped = shaped.transpose(0, 3, 1, 2, 4, 5)
    return shaped.reshape(-1, 2 * CLAT * levels * WLON, channels)

def from_windows(tensor, latitude, longitude):
    channels = tensor.shape[-1]
    shaped = tensor.reshape(latitude // (2 * CLAT), longitude // WLON, 2 * CLAT, LEV, WLON, channels)
    shaped = shaped.transpose(0, 2, 3, 1, 4, 5)
    return shaped.reshape(latitude, LEV, longitude, channels)

def reference(tokens, norm_gain, w_qkv, w_out, grad_out):
    latitude = tokens.shape[0]
    longitude = tokens.shape[2]
    offset = WLON // 2
    heads_dev = D // N_OUTER
    score_scale = HEAD ** (-0.5)
    standard, inverse_std = normalize(tokens)
    normed = (standard * norm_gain).astype(jnp.bfloat16)
    rolled = jnp.roll(normed, (-CLAT, -offset), axis=(0, 2))
    window_in = to_windows(rolled)
    window_count = window_in.shape[0]
    window_size = window_in.shape[1]
    lon_blocks = longitude // WLON
    lat_blocks = latitude // (2 * CLAT)
    wrapped = jnp.arange(window_count) >= (lat_blocks - 1) * lon_blocks
    half_index = jnp.arange(window_size) // (CLAT * LEV * WLON)
    same_half = half_index[:, None] == half_index[None, :]
    allowed = jnp.logical_or(jnp.logical_not(wrapped)[:, None, None], same_half[None])
    flat_in = window_in.reshape(-1, D)
    w_flat = w_qkv.reshape(D, 3 * D)
    projected = jnp.dot(flat_in, w_flat, preferred_element_type=jnp.float32).astype(jnp.bfloat16)
    projected = projected.reshape(window_count, window_size, 3, HEADS, HEAD).astype(jnp.float32)
    queries = projected[:, :, 0]
    keys_all = projected[:, :, 1]
    values = projected[:, :, 2]
    scores = jnp.einsum('nqhd,nkhd->nhqk', queries, keys_all) * score_scale
    scores = jnp.where(allowed[:, None], scores, -1e+30)
    softmax_weights = jax.nn.softmax(scores, axis=-1)
    weights_low = softmax_weights.astype(jnp.bfloat16).astype(jnp.float32)
    attended = jnp.einsum('nhqk,nkhd->nqhd', weights_low, values).astype(jnp.bfloat16).reshape(-1, D)
    branch = jnp.zeros((attended.shape[0], D), jnp.float32)
    for group_index in range(N_OUTER):
        lower = group_index * heads_dev
        partial_term = jnp.dot(attended[:, lower:lower + heads_dev], w_out[lower:lower + heads_dev], preferred_element_type=jnp.float32)
        branch = branch + lax.optimization_barrier(partial_term.astype(jnp.bfloat16)).astype(jnp.float32)
    branch_low = from_windows(branch.astype(jnp.bfloat16).reshape(window_count, window_size, D), latitude, longitude)
    branch_low = jnp.roll(branch_low, (CLAT, offset), axis=(0, 2))
    output = (tokens.astype(jnp.float32) + branch_low.astype(jnp.float32)).astype(jnp.bfloat16)
    cotangent = jnp.roll(grad_out, (-CLAT, -offset), axis=(0, 2))
    cot_flat = to_windows(cotangent).reshape(-1, D)
    grad_wout = jnp.dot(attended.T, cot_flat, preferred_element_type=jnp.float32)
    d_attended = jnp.dot(cot_flat, w_out.T, preferred_element_type=jnp.float32).astype(jnp.bfloat16)
    d_window = d_attended.reshape(window_count, window_size, HEADS, HEAD).astype(jnp.float32)
    d_weights = jnp.einsum('nqhd,nkhd->nhqk', d_window, values)
    row_dots = lax.optimization_barrier(jnp.sum(softmax_weights * d_weights, -1, keepdims=True))
    d_scores = (softmax_weights * (d_weights - row_dots) * score_scale).astype(jnp.bfloat16).astype(jnp.float32)
    d_query = jnp.einsum('nhqk,nkhd->nqhd', d_scores, keys_all)
    d_key = jnp.einsum('nhqk,nqhd->nkhd', d_scores, queries)
    d_value = jnp.einsum('nhqk,nqhd->nkhd', weights_low, d_window)
    d_projected = jnp.stack([d_query, d_key, d_value], axis=2).astype(jnp.bfloat16).reshape(-1, 3 * D)
    grad_wqkv = jnp.dot(flat_in.T, d_projected, preferred_element_type=jnp.float32).reshape(D, 3, D)
    d_three = d_projected.reshape(-1, 3, D)
    d_rolled = jnp.zeros((d_three.shape[0], D), jnp.float32)
    for group_index in range(N_OUTER):
        lower = group_index * heads_dev
        d_group = d_three[:, :, lower:lower + heads_dev].reshape(-1, 3 * heads_dev)
        w_group = w_qkv[:, :, lower:lower + heads_dev].reshape(D, 3 * heads_dev)
        partial_term = jnp.dot(d_group, w_group.T, preferred_element_type=jnp.float32)
        d_rolled = d_rolled + lax.optimization_barrier(partial_term.astype(jnp.bfloat16)).astype(jnp.float32)
    d_normed = from_windows(d_rolled.astype(jnp.bfloat16).reshape(window_count, window_size, D), latitude, longitude)
    d_normed = jnp.roll(d_normed, (CLAT, offset), axis=(0, 2)).astype(jnp.float32)
    grad_gain = lax.optimization_barrier(jnp.sum((d_normed * standard).reshape(-1, D), 0))
    scaled = d_normed * norm_gain
    d_local = inverse_std * (scaled - lax.optimization_barrier(jnp.mean(scaled, -1, keepdims=True)) - standard * lax.optimization_barrier(jnp.mean(scaled * standard, -1, keepdims=True)))
    grad_tokens = (grad_out.astype(jnp.float32) + d_local).astype(jnp.bfloat16)
    return (output, grad_tokens, grad_wqkv, grad_wout, grad_gain)
```

```python
import functools

import jax
import jax.numpy as jnp
from jax import lax
from jax.experimental import pallas as pl
from jax.experimental.pallas import tpu as pltpu
from jax.sharding import PartitionSpec as P

D = 2048
HEAD = 64
LEV = 2
CLAT = 3
WLON = 12
QUARTER = CLAT * LEV * WLON // 2
PAIR = 80
MESH = pl.DeviceIdType.MESH
epsilon = 1e-05


def position():
    return lax.axis_index("outer"), lax.axis_index("lat"), lax.axis_index("lon")


def enter(receivers, senders):
    barrier = pltpu.get_barrier_semaphore()
    for device in senders:
        pl.semaphore_signal(barrier, inc=1, device_id=device, device_id_type=MESH)
    pl.semaphore_wait(barrier, len(receivers))


def shifted(sizes, band, lat, lon, rows, columns):
    replicas, n_lat, n_lon = sizes
    flat = lax.rem(band * n_lat + lat + rows + replicas * n_lat, replicas * n_lat)
    return flat // n_lat, lax.rem(flat, n_lat), lax.rem(lon + columns + n_lon, n_lon)


def gather_routes(sizes):
    outer, lat, lon = position()
    routes = []
    for step in range(sizes[0]):
        for a in range(2):
            for b in range(2):
                band, lat_to, lon_to = shifted(sizes, outer, lat, lon, -a, -b)
                group = lax.rem(band + step, sizes[0])
                band_from, lat_from, lon_from = shifted(sizes, outer, lat, lon, a, b)
                tile_from = lax.rem(outer - step + sizes[0], sizes[0])
                source_band, source_lat, source_lon = shifted(sizes, tile_from, lat, lon, a, b)
                routes.append(
                    (
                        step,
                        2 * a + b,
                        (group, lat_to, lon_to),
                        band,
                        (source_band, source_lat, source_lon),
                        tile_from,
                    )
                )
    return routes


def front_kernel(sizes, src, got, send_sem, recv_sem, local_sem):
    routes = gather_routes(sizes)
    remote = [r for r in routes if (r[0], r[1]) != (0, 0)]
    enter([r[2] for r in remote], [r[4] for r in remote])
    outer, _, _ = position()
    copies = []
    for index, (step, block, target, tile, _, tile_from) in enumerate(remote):
        push = pltpu.make_async_remote_copy(
            src.at[block],
            got.at[tile, block],
            send_sem.at[index],
            recv_sem.at[index],
            device_id=target,
            device_id_type=MESH,
        )
        push.start()
        arrive = pltpu.make_async_remote_copy(
            src.at[block],
            got.at[tile_from, block],
            send_sem.at[index],
            recv_sem.at[index],
            device_id=target,
            device_id_type=MESH,
        )
        copies.append((push, arrive))
    own = pltpu.make_async_copy(src.at[0], got.at[outer, 0], local_sem)
    own.start()
    for push, arrive in copies:
        arrive.wait_recv()
    for push, arrive in copies:
        push.wait_send()
    own.wait()


def front_exchange(sizes, blocks):
    replicas = sizes[0]
    count = 4 * replicas - 1
    return pl.pallas_call(
        functools.partial(front_kernel, sizes),
        out_shape=jax.ShapeDtypeStruct((replicas, 4, PAIR, D), jnp.bfloat16),
        in_specs=[pl.BlockSpec(memory_space=pl.ANY)],
        out_specs=pl.BlockSpec(memory_space=pl.ANY),
        scratch_shapes=[
            pltpu.SemaphoreType.DMA((count,)),
            pltpu.SemaphoreType.DMA((count,)),
            pltpu.SemaphoreType.DMA(()),
        ],
        compiler_params=pltpu.CompilerParams(collective_id=1, has_side_effects=True),
    )(blocks)


def back_routes(sizes):
    outer, lat, lon = position()
    routes = []
    for step in range(sizes[0]):
        for a in range(2):
            for b in range(2):
                tile = lax.rem(outer + step, sizes[0])
                target = shifted(sizes, tile, lat, lon, a, b)
                band, lat_from, lon_from = shifted(sizes, outer, lat, lon, -a, -b)
                group_from = lax.rem(band - step + sizes[0], sizes[0])
                routes.append((step, 2 * a + b, tile, target, (group_from, lat_from, lon_from)))
    return routes


def xor_partners(sizes):
    outer, lat, lon = position()
    result = []
    for axis, size in enumerate(sizes):
        bit = 1
        while bit < size:
            at = [outer, lat, lon]
            lower = lax.rem(at[axis] // bit, 2)
            at[axis] = at[axis] + bit * (1 - 2 * lower)
            result.append(tuple(at))
            bit *= 2
    return result


def grads_kernel(
    sizes,
    x_ref,
    y_ref,
    gain_ref,
    back_ref,
    total_ref,
    got_ref,
    gain_out,
    x_pair,
    y_pair,
    first,
    slots,
    own,
    gain_acc,
    gain_slots,
    pair_send,
    pair_recv,
    rs_send,
    rs_recv,
    ag_send,
    ag_recv,
    share_send,
    share_recv,
    back_send,
    back_recv,
    gain_send,
    gain_recv,
    local_sem,
):
    replicas, n_lat, n_lon = sizes
    outer, lat, lon = position()
    count = n_lat // 2 * n_lon
    rows = D // 2 // count
    half = lax.rem(lat, 2)
    upper = lat // 2
    partner = (outer, lat + 1 - 2 * half, lon)

    def on_ring(place):
        place = lax.rem(place + count, count)
        turned = jnp.where(half == 0, place, count - 1 - place)
        row = turned // n_lon
        column = lax.rem(turned, n_lon)
        return (outer, 2 * row + half, jnp.where(lax.rem(row, 2) == 0, column, n_lon - 1 - column))

    along = jnp.where(lax.rem(upper, 2) == 0, lon, n_lon - 1 - lon)
    spot = upper * n_lon + along
    me = jnp.where(half == 0, spot, count - 1 - spot)
    after, before = on_ring(me + 1), on_ring(me - 1)

    routes = [r for r in back_routes(sizes) if (r[0], r[1]) != (0, 0)]
    friends = xor_partners(sizes)
    enter(
        [after, partner] + [r[3] for r in routes] + friends,
        [before, partner] + [r[4] for r in routes] + friends,
    )

    def remote(src, dst, send, recv, device):
        return pltpu.make_async_remote_copy(
            src, dst, send, recv, device_id=device, device_id_type=MESH
        )

    half_d = D // 2
    theirs = pl.ds(pl.multiple_of((1 - half) * half_d, half_d), half_d)
    swap_x = remote(x_ref.at[:, :, theirs], x_pair, pair_send.at[0], pair_recv.at[0], partner)
    swap_y = remote(y_ref, y_pair, pair_send.at[1], pair_recv.at[1], partner)
    swap_x.start()
    swap_y.start()

    back = []
    for index, (step, block, tile, target, _) in enumerate(routes):
        push = remote(
            back_ref.at[tile, block],
            got_ref.at[step, block],
            back_send.at[index],
            back_recv.at[index],
            target,
        )
        push.start()
        back.append(push)
    keep = pltpu.make_async_copy(back_ref.at[outer, 0], got_ref.at[0, 0], local_sem.at[4])
    keep.start()

    swap_x.wait_recv()
    swap_y.wait_recv()

    contract = (((0,), (0,)), ((), ()))

    def product(chunk, part):
        which = 0 if part < 3 else 1
        here = pl.ds(pl.multiple_of(half * half_d + chunk * rows, rows), rows)
        there = pl.ds(pl.multiple_of(chunk * rows, rows), rows)
        mine = lax.dot_general(
            x_ref[which, :, here], y_ref[part], contract, preferred_element_type=jnp.float32
        )
        other = lax.dot_general(
            x_pair[which, :, there], y_pair[part], contract, preferred_element_type=jnp.float32
        )
        return mine + other

    def ring_copy(src, step, part):
        return remote(
            src.at[part], slots.at[step, part], rs_send.at[step, part], rs_recv.at[step, part], after
        )

    for part in range(4):
        first[part] = product(me, part).astype(jnp.bfloat16)
        ring_copy(first, 0, part).start()

    def reduce_step(step, carry):
        chunk = lax.rem(me - step - 1 + count, count)
        for part in range(4):
            own[part] = product(chunk, part)
        for part in range(4):
            ring_copy(first, step, part).wait_recv()
            slots[step, part] = (slots[step, part].astype(jnp.float32) + own[part]).astype(
                jnp.bfloat16
            )

            @pl.when(step < count - 2)
            def _():
                ring_copy(slots.at[step], step + 1, part).start()

        return carry

    lax.fori_loop(0, count - 1, reduce_step, 0)

    def place(chunk, part):
        start = pl.multiple_of(half * half_d + chunk * rows, rows)
        return total_ref.at[part, pl.ds(start, rows)]

    def other_place(chunk, part):
        start = pl.multiple_of((1 - half) * half_d + chunk * rows, rows)
        return total_ref.at[part, pl.ds(start, rows)]

    done = lax.rem(me + 1, count)
    final = slots.at[count - 2]
    pending = []
    for part in range(4):
        spread = remote(
            final.at[part], place(done, part), ag_send.at[0, part], ag_recv.at[0, part], after
        )
        spread.start()
        share = remote(
            final.at[part], place(done, part), share_send.at[0, part], share_recv.at[0, part], partner
        )
        share.start()
        store = pltpu.make_async_copy(final.at[part], place(done, part), local_sem.at[part])
        store.start()
        pending.append((spread, share, store))

    def gain_copy(step):
        return remote(
            gain_acc.at[step],
            gain_slots.at[step],
            gain_send.at[step],
            gain_recv.at[step],
            friends[step],
        )

    gain_acc[0] = gain_ref[...]
    gain_copy(0).start()
    rounds = len(friends)

    def gain_round(step):
        gain_copy(step).wait_recv()
        gain_acc[step + 1] = gain_acc[step] + gain_slots[step]
        if step + 1 < rounds:
            gain_copy(step + 1).start()

    sends = []
    for step in range(count - 1):
        chunk = lax.rem(me - step + count, count)
        for part in range(4):
            spot_ref = place(chunk, part)
            remote(
                final.at[part], spot_ref, ag_send.at[step, part], ag_recv.at[step, part], after
            ).wait_recv()
            if step < count - 2:
                spread = remote(
                    spot_ref, spot_ref, ag_send.at[step + 1, part], ag_recv.at[step + 1, part], after
                )
                spread.start()
                sends.append(spread)
            share = remote(
                spot_ref,
                spot_ref,
                share_send.at[step + 1, part],
                share_recv.at[step + 1, part],
                partner,
            )
            share.start()
            sends.append(share)
        if step < rounds:
            gain_round(step)
    for step in range(count - 1, rounds):
        gain_round(step)
    gain_out[...] = gain_acc[rounds]

    partner_me = jnp.where(half == 0, count - 1 - spot, spot)
    for step in range(count):
        chunk = lax.rem(partner_me + 1 - step + count, count)
        for part in range(4):
            remote(
                final.at[part],
                other_place(chunk, part),
                share_send.at[step, part],
                share_recv.at[step, part],
                partner,
            ).wait_recv()
    for index, (step, block, tile, target, _) in enumerate(routes):
        back[index].wait_recv()
        back[index].wait_send()
    keep.wait()
    swap_x.wait_send()
    swap_y.wait_send()
    for part in range(4):
        ring_copy(first, 0, part).wait_send()

    def drain(step, carry):
        for part in range(4):
            ring_copy(slots.at[step], step + 1, part).wait_send()
        return carry

    lax.fori_loop(0, count - 2, drain, 0)
    for spread, share, store in pending:
        spread.wait_send()
        share.wait_send()
        store.wait()
    for copy in sends:
        copy.wait_send()
    for step in range(rounds):
        gain_copy(step).wait_send()


def grads_exchange(sizes, x, y, gain, back):
    replicas, n_lat, n_lon = sizes
    count = n_lat // 2 * n_lon
    rows = D // 2 // count
    tokens, heads_dev = y.shape[1:]
    friends = sum(size.bit_length() - 1 for size in sizes)
    routes = 4 * replicas - 1
    dma = pltpu.SemaphoreType.DMA
    vmem = pl.BlockSpec(memory_space=pltpu.VMEM)
    hbm = pl.BlockSpec(memory_space=pl.ANY)
    return pl.pallas_call(
        functools.partial(grads_kernel, sizes),
        out_shape=(
            jax.ShapeDtypeStruct((4, D, heads_dev), jnp.bfloat16),
            jax.ShapeDtypeStruct((replicas, 4, PAIR, D), jnp.bfloat16),
            jax.ShapeDtypeStruct((D // 128, 128), jnp.float32),
        ),
        in_specs=[vmem, vmem, vmem, hbm],
        out_specs=(hbm, hbm, vmem),
        scratch_shapes=[
            pltpu.VMEM((2, tokens, D // 2), jnp.bfloat16),
            pltpu.VMEM((4, tokens, heads_dev), jnp.bfloat16),
            pltpu.VMEM((4, rows, heads_dev), jnp.bfloat16),
            pltpu.VMEM((count - 1, 4, rows, heads_dev), jnp.bfloat16),
            pltpu.VMEM((4, rows, heads_dev), jnp.float32),
            pltpu.VMEM((friends + 1, D // 128, 128), jnp.float32),
            pltpu.VMEM((friends, D // 128, 128), jnp.float32),
            dma((2,)),
            dma((2,)),
            dma((count - 1, 4)),
            dma((count - 1, 4)),
            dma((count - 1, 4)),
            dma((count - 1, 4)),
            dma((count, 4)),
            dma((count, 4)),
            dma((routes,)),
            dma((routes,)),
            dma((friends,)),
            dma((friends,)),
            dma((5,)),
        ],
        compiler_params=pltpu.CompilerParams(
            collective_id=2, has_side_effects=True, vmem_limit_bytes=56 * 1024 * 1024
        ),
    )(x, y, gain, back)


def normalize(tokens):
    values_f = tokens.astype(jnp.float32)
    average = jnp.mean(values_f, -1, keepdims=True)
    centered = values_f - average
    inverse_std = lax.rsqrt(jnp.mean(centered * centered, -1, keepdims=True) + epsilon)
    return (centered * inverse_std, inverse_std)


def contract_cols(left, right):
    return lax.dot_general(
        left, right, (((1,), (1,)), ((), ())), preferred_element_type=jnp.float32
    )


def to_blocks(tensor):
    shaped = tensor.reshape(2, CLAT, 2, WLON // 2, LEV, D)
    blocks = [shaped[1 - a, :, 1 - b].reshape(QUARTER, D) for a in range(2) for b in range(2)]
    return jnp.stack(blocks)


def from_blocks(blocks):
    shaped = blocks.reshape(2, 2, CLAT, WLON // 2, LEV, D)
    rows = [jnp.concatenate([shaped[a, 1], shaped[a, 0]], axis=1) for a in (1, 0)]
    return jnp.concatenate(rows, axis=0)


def shards(tokens, norm_gain, w_qkv, w_out, grad_out):
    sizes = tuple(lax.axis_size(name) for name in ("outer", "lat", "lon"))
    replicas, lat_count, lon_count = sizes
    assert tokens.shape[:3] == (2 * CLAT, LEV, WLON)
    lat_index = lax.axis_index("lat")
    heads_dev = w_qkv.shape[2]
    head_count = heads_dev // HEAD
    score_scale = HEAD ** (-0.5)
    window_size = 4 * QUARTER
    total = replicas * window_size
    w_three = w_qkv.transpose(1, 0, 2)
    tokens_n = tokens.transpose(0, 2, 1, 3)
    grad_n = grad_out.transpose(0, 2, 1, 3)
    standard, inverse_std = normalize(tokens_n)
    normed = (standard * norm_gain).astype(jnp.bfloat16)
    filler = jnp.zeros((4, PAIR - 2 * QUARTER, D), jnp.bfloat16)
    sent = jnp.concatenate([to_blocks(normed), to_blocks(grad_n), filler], axis=1)
    arrived = front_exchange(sizes, sent)
    gathered = arrived[:, :, :QUARTER].reshape(total, D)
    cot_all = arrived[:, :, QUARTER : 2 * QUARTER].reshape(total, D)

    def heads(tensor):
        return tensor.reshape(replicas, window_size, head_count, HEAD)

    queries, keys_all, values = [
        heads(
            jnp.dot(gathered, w_three[i], preferred_element_type=jnp.float32).astype(jnp.bfloat16)
        )
        for i in range(3)
    ]
    cut_window = jnp.logical_and(lat_index == lat_count - 1, jnp.arange(replicas) == replicas - 1)
    half_index = jnp.arange(window_size) // (2 * QUARTER)
    same_half = half_index[:, None] == half_index[None, :]
    allowed = jnp.logical_or(jnp.logical_not(cut_window)[:, None, None], same_half[None])
    scores = (
        jnp.einsum("wqhd,wkhd->whqk", queries, keys_all, preferred_element_type=jnp.float32)
        * score_scale
    )
    scores = jnp.where(allowed[:, None], scores, -1e30)
    largest = jnp.max(scores, -1, keepdims=True)
    exponent = jnp.exp(scores - largest)
    softmax_weights = exponent / jnp.sum(exponent, -1, keepdims=True)
    weights_low = softmax_weights.astype(jnp.bfloat16)
    attended = jnp.einsum(
        "whqk,wkhd->wqhd", weights_low, values, preferred_element_type=jnp.float32
    )
    attended = attended.astype(jnp.bfloat16).reshape(total, heads_dev)
    branch = jnp.dot(attended, w_out, preferred_element_type=jnp.float32).astype(jnp.bfloat16)
    d_window = heads(contract_cols(cot_all, w_out).astype(jnp.bfloat16))
    d_weights = jnp.einsum("wqhd,wkhd->whqk", d_window, values, preferred_element_type=jnp.float32)
    row_dots = jnp.sum(softmax_weights * d_weights, -1, keepdims=True)
    d_scores = (softmax_weights * (d_weights - row_dots) * score_scale).astype(jnp.bfloat16)
    d_query = jnp.einsum("whqk,wkhd->wqhd", d_scores, keys_all, preferred_element_type=jnp.float32)
    d_key = jnp.einsum("whqk,wqhd->wkhd", d_scores, queries, preferred_element_type=jnp.float32)
    d_value = jnp.einsum(
        "whqk,wqhd->wkhd", weights_low, d_window, preferred_element_type=jnp.float32
    )
    d_parts = [
        part.astype(jnp.bfloat16).reshape(total, heads_dev) for part in (d_query, d_key, d_value)
    ]
    d_rolled = sum(contract_cols(d_parts[i], w_three[i]) for i in range(3)).astype(jnp.bfloat16)
    gain_local = (
        jnp.sum(d_rolled.astype(jnp.float32) * gathered.astype(jnp.float32), 0) / norm_gain
    )
    in_blocks = (replicas, 4, QUARTER, D)
    back = jnp.concatenate(
        [
            branch.reshape(in_blocks),
            d_rolled.reshape(in_blocks),
            jnp.zeros((replicas, 4, PAIR - 2 * QUARTER, D), jnp.bfloat16),
        ],
        axis=2,
    )
    grads, returned, grad_gain = grads_exchange(
        sizes,
        jnp.stack([gathered, cot_all]),
        jnp.stack(d_parts + [attended]),
        gain_local.reshape(D // 128, 128),
        back,
    )
    summed = jnp.sum(returned.astype(jnp.float32), 0).astype(jnp.bfloat16)
    branch_low = from_blocks(summed[:, :QUARTER])
    d_normed = from_blocks(summed[:, QUARTER : 2 * QUARTER]).astype(jnp.float32)
    output = (tokens_n.astype(jnp.float32) + branch_low.astype(jnp.float32)).astype(jnp.bfloat16)
    scaled = d_normed * norm_gain
    d_local = inverse_std * (
        scaled
        - jnp.mean(scaled, -1, keepdims=True)
        - standard * jnp.mean(scaled * standard, -1, keepdims=True)
    )
    grad_tokens = (grad_n.astype(jnp.float32) + d_local).astype(jnp.bfloat16)
    grad_wqkv = grads[:3].astype(jnp.float32).transpose(1, 0, 2)
    grad_wout = grads[3].astype(jnp.float32).T
    return (
        output.transpose(0, 2, 1, 3),
        grad_tokens.transpose(0, 2, 1, 3),
        grad_wqkv,
        grad_wout,
        grad_gain.reshape(D),
    )


def solution(mesh):
    in_specs = (
        P(("outer", "lat"), None, "lon", None),
        P(),
        P(None, None, "outer"),
        P("outer", None),
        P(("outer", "lat"), None, "lon", None),
    )
    out_specs = (
        P(("outer", "lat"), None, "lon", None),
        P(("outer", "lat"), None, "lon", None),
        P(None, None, "outer"),
        P("outer", None),
        P(),
    )
    return jax.shard_map(shards, mesh=mesh, in_specs=in_specs, out_specs=out_specs, check_vma=False)
```

```python
import functools

import jax
import jax.numpy as jnp
from jax import lax
from jax.experimental import pallas as pl
from jax.experimental.pallas import tpu as pltpu
from jax.sharding import PartitionSpec as P

D = 2048
HEAD = 64
LEV = 2
CLAT = 3
WLON = 12
QUARTER = CLAT * LEV * WLON // 2
PAIR = 80
MESH = pl.DeviceIdType.MESH
epsilon = 1e-05


def position():
    return lax.axis_index("outer"), lax.axis_index("lat"), lax.axis_index("lon")


def enter(receivers, senders):
    barrier = pltpu.get_barrier_semaphore()
    for device in senders:
        pl.semaphore_signal(barrier, inc=1, device_id=device, device_id_type=MESH)
    pl.semaphore_wait(barrier, len(receivers))


def shifted(sizes, band, lat, lon, rows, columns):
    replicas, n_lat, n_lon = sizes
    flat = lax.rem(band * n_lat + lat + rows + replicas * n_lat, replicas * n_lat)
    return flat // n_lat, lax.rem(flat, n_lat), lax.rem(lon + columns + n_lon, n_lon)


def gather_routes(sizes):
    outer, lat, lon = position()
    routes = []
    for step in range(sizes[0]):
        for a in range(2):
            for b in range(2):
                band, lat_to, lon_to = shifted(sizes, outer, lat, lon, -a, -b)
                group = lax.rem(band + step, sizes[0])
                band_from, lat_from, lon_from = shifted(sizes, outer, lat, lon, a, b)
                tile_from = lax.rem(outer - step + sizes[0], sizes[0])
                source_band, source_lat, source_lon = shifted(sizes, tile_from, lat, lon, a, b)
                routes.append(
                    (
                        step,
                        2 * a + b,
                        (group, lat_to, lon_to),
                        band,
                        (source_band, source_lat, source_lon),
                        tile_from,
                    )
                )
    return routes


def front_kernel(sizes, src, got, send_sem, recv_sem, local_sem):
    routes = gather_routes(sizes)
    remote = [r for r in routes if (r[0], r[1]) != (0, 0)]
    enter([r[2] for r in remote], [r[4] for r in remote])
    outer, _, _ = position()
    copies = []
    for index, (step, block, target, tile, _, tile_from) in enumerate(remote):
        push = pltpu.make_async_remote_copy(
            src.at[block],
            got.at[tile, block],
            send_sem.at[index],
            recv_sem.at[index],
            device_id=target,
            device_id_type=MESH,
        )
        push.start()
        arrive = pltpu.make_async_remote_copy(
            src.at[block],
            got.at[tile_from, block],
            send_sem.at[index],
            recv_sem.at[index],
            device_id=target,
            device_id_type=MESH,
        )
        copies.append((push, arrive))
    own = pltpu.make_async_copy(src.at[0], got.at[outer, 0], local_sem)
    own.start()
    for push, arrive in copies:
        arrive.wait_recv()
    for push, arrive in copies:
        push.wait_send()
    own.wait()


def front_exchange(sizes, blocks):
    replicas = sizes[0]
    count = 4 * replicas - 1
    return pl.pallas_call(
        functools.partial(front_kernel, sizes),
        out_shape=jax.ShapeDtypeStruct((replicas, 4, PAIR, D), jnp.bfloat16),
        in_specs=[pl.BlockSpec(memory_space=pl.ANY)],
        out_specs=pl.BlockSpec(memory_space=pl.ANY),
        scratch_shapes=[
            pltpu.SemaphoreType.DMA((count,)),
            pltpu.SemaphoreType.DMA((count,)),
            pltpu.SemaphoreType.DMA(()),
        ],
        compiler_params=pltpu.CompilerParams(collective_id=1, has_side_effects=True),
    )(blocks)


def xor_partners(sizes):
    outer, lat, lon = position()
    result = []
    for axis, size in enumerate(sizes):
        bit = 1
        while bit < size:
            at = [outer, lat, lon]
            lower = lax.rem(at[axis] // bit, 2)
            at[axis] = at[axis] + bit * (1 - 2 * lower)
            result.append(tuple(at))
            bit *= 2
    return result


def grads_kernel(
    sizes,
    x_ref,
    c_ref,
    y_ref,
    gain_ref,
    back_ref,
    qkv_ref,
    out_ref,
    shares_ref,
    got_ref,
    gain_out,
    x_pair,
    c_pair,
    y_pair,
    first_q,
    first_o,
    slots_q,
    slots_o,
    own_q,
    own_o,
    gain_acc,
    gain_slots,
    tile_in,
    tile_sum,
    tile_low,
    pair_send,
    pair_recv,
    rs_send,
    rs_recv,
    ag_send,
    ag_recv,
    share_send,
    share_recv,
    outer_send,
    outer_recv,
    back_send,
    back_recv,
    gain_send,
    gain_recv,
    local_sem,
):
    replicas, n_lat, n_lon = sizes
    outer, lat, lon = position()
    count = n_lat // 2 * n_lon
    rows = D // 2 // count
    half = lax.rem(lat, 2)
    upper = lat // 2
    partner = (outer, lat + 1 - 2 * half, lon)

    def on_ring(place):
        place = lax.rem(place + count, count)
        turned = jnp.where(half == 0, place, count - 1 - place)
        row = turned // n_lon
        column = lax.rem(turned, n_lon)
        return (outer, 2 * row + half, jnp.where(lax.rem(row, 2) == 0, column, n_lon - 1 - column))

    along = jnp.where(lax.rem(upper, 2) == 0, lon, n_lon - 1 - lon)
    spot = upper * n_lon + along
    me = jnp.where(half == 0, spot, count - 1 - spot)
    after, before = on_ring(me + 1), on_ring(me - 1)

    groups_to = [(lax.rem(outer + step, replicas), lat, lon) for step in range(1, replicas)]
    groups_from = [
        (lax.rem(outer - step + replicas, replicas), lat, lon) for step in range(1, replicas)
    ]
    moves = [(0, 1), (1, 0), (1, 1)]
    halo_to = [shifted(sizes, outer, lat, lon, a, b) for a, b in moves]
    halo_from = [shifted(sizes, outer, lat, lon, -a, -b) for a, b in moves]
    friends = xor_partners(sizes)
    enter(
        [after, partner] + groups_to + halo_to + friends,
        [before, partner] + groups_from + halo_from + friends,
    )

    def remote(src, dst, send, recv, device):
        return pltpu.make_async_remote_copy(
            src, dst, send, recv, device_id=device, device_id_type=MESH
        )

    half_d = D // 2
    theirs = pl.ds(pl.multiple_of((1 - half) * half_d, half_d), half_d)
    swaps = [
        remote(x_ref.at[:, theirs], x_pair, pair_send.at[0], pair_recv.at[0], partner),
        remote(y_ref, y_pair, pair_send.at[1], pair_recv.at[1], partner),
        remote(c_ref.at[:, theirs], c_pair, pair_send.at[2], pair_recv.at[2], partner),
    ]
    for swap in swaps:
        swap.start()
    back = []
    for index, target in enumerate(groups_to):
        push = remote(
            back_ref.at[target[0]],
            shares_ref.at[index],
            outer_send.at[index],
            outer_recv.at[index],
            target,
        )
        push.start()
        back.append(push)
    for swap in swaps:
        swap.wait_recv()

    contract = (((0,), (0,)), ((), ()))

    def product(chunk, part):
        here = pl.ds(pl.multiple_of(half * half_d + chunk * rows, rows), rows)
        there = pl.ds(pl.multiple_of(chunk * rows, rows), rows)
        if part < 3:
            pairs = [(x_ref[:, here], y_ref[part]), (x_pair[:, there], y_pair[part])]
        else:
            pairs = [(y_ref[3], c_ref[:, here]), (y_pair[3], c_pair[:, there])]
        mine, other = [
            lax.dot_general(left, right, contract, preferred_element_type=jnp.float32)
            for left, right in pairs
        ]
        return mine + other

    def first_at(part):
        return first_q.at[part] if part < 3 else first_o

    def own_at(part):
        return own_q.at[part] if part < 3 else own_o

    def slot_at(step, part):
        return slots_q.at[step, part] if part < 3 else slots_o.at[step]

    def ring_copy(src, step, part):
        return remote(
            src, slot_at(step, part), rs_send.at[step, part], rs_recv.at[step, part], after
        )

    for part in range(4):
        first_at(part)[...] = product(me, part).astype(jnp.bfloat16)
        ring_copy(first_at(part), 0, part).start()

    def reduce_step(step, carry):
        chunk = lax.rem(me - step - 1 + count, count)
        for part in range(4):
            own_at(part)[...] = product(chunk, part)
        for part in range(4):
            slot = slot_at(step, part)
            ring_copy(first_at(part), step, part).wait_recv()
            slot[...] = (slot[...].astype(jnp.float32) + own_at(part)[...]).astype(jnp.bfloat16)

            @pl.when(step < count - 2)
            def _():
                ring_copy(slot_at(step, part), step + 1, part).start()

        return carry

    lax.fori_loop(0, count - 1, reduce_step, 0)

    def place(side, chunk, part):
        start = pl.multiple_of(side * half_d + chunk * rows, rows)
        if part < 3:
            return qkv_ref.at[part, pl.ds(start, rows)]
        return out_ref.at[:, pl.ds(start, rows)]

    done = lax.rem(me + 1, count)
    pending = []
    for part in range(4):
        final = slot_at(count - 2, part)
        target = place(half, done, part)
        spread = remote(final, target, ag_send.at[0, part], ag_recv.at[0, part], after)
        spread.start()
        share = remote(final, target, share_send.at[0, part], share_recv.at[0, part], partner)
        share.start()
        store = pltpu.make_async_copy(final, target, local_sem.at[part])
        store.start()
        pending.append((spread, share, store))

    def gain_copy(step):
        return remote(
            gain_acc.at[step],
            gain_slots.at[step],
            gain_send.at[step],
            gain_recv.at[step],
            friends[step],
        )

    gain_acc[0] = gain_ref[...]
    gain_copy(0).start()
    rounds = len(friends)

    def gain_round(step):
        gain_copy(step).wait_recv()
        gain_acc[step + 1] = gain_acc[step] + gain_slots[step]
        if step + 1 < rounds:
            gain_copy(step + 1).start()

    load = pltpu.make_async_copy(back_ref.at[outer], tile_in, local_sem.at[4])
    load.start()
    load.wait()
    tile_sum[...] = tile_in[...].astype(jnp.float32)
    for index in range(replicas - 1):
        back[index].wait_recv()
        load = pltpu.make_async_copy(shares_ref.at[index], tile_in, local_sem.at[5])
        load.start()
        load.wait()
        tile_sum[...] += tile_in[...].astype(jnp.float32)
    tile_low[...] = tile_sum[...].astype(jnp.bfloat16)
    keep = pltpu.make_async_copy(tile_low.at[0], got_ref.at[0], local_sem.at[6])
    keep.start()
    halos = []
    for index, (a, b) in enumerate(moves):
        block = 2 * a + b
        push = remote(
            tile_low.at[block],
            got_ref.at[block],
            back_send.at[index],
            back_recv.at[index],
            halo_to[index],
        )
        push.start()
        halos.append(push)

    sends = []
    for step in range(count - 1):
        chunk = lax.rem(me - step + count, count)
        for part in range(4):
            here = place(half, chunk, part)
            remote(
                slot_at(count - 2, part), here, ag_send.at[step, part], ag_recv.at[step, part], after
            ).wait_recv()
            if step < count - 2:
                spread = remote(
                    here, here, ag_send.at[step + 1, part], ag_recv.at[step + 1, part], after
                )
                spread.start()
                sends.append(spread)
            share = remote(
                here, here, share_send.at[step + 1, part], share_recv.at[step + 1, part], partner
            )
            share.start()
            sends.append(share)
        if step < rounds:
            gain_round(step)
    for step in range(count - 1, rounds):
        gain_round(step)
    gain_out[...] = gain_acc[rounds]

    partner_me = jnp.where(half == 0, count - 1 - spot, spot)
    for step in range(count):
        chunk = lax.rem(partner_me + 1 - step + count, count)
        for part in range(4):
            remote(
                slot_at(count - 2, part),
                place(1 - half, chunk, part),
                share_send.at[step, part],
                share_recv.at[step, part],
                partner,
            ).wait_recv()
    for push in halos:
        push.wait_recv()
        push.wait_send()
    keep.wait()
    for push in back:
        push.wait_send()
    for swap in swaps:
        swap.wait_send()
    for part in range(4):
        ring_copy(first_at(part), 0, part).wait_send()

    def drain(step, carry):
        for part in range(4):
            ring_copy(slot_at(step, part), step + 1, part).wait_send()
        return carry

    lax.fori_loop(0, count - 2, drain, 0)
    for spread, share, store in pending:
        spread.wait_send()
        share.wait_send()
        store.wait()
    for copy in sends:
        copy.wait_send()
    for step in range(rounds):
        gain_copy(step).wait_send()


def grads_exchange(sizes, x, c, y, gain, back):
    replicas, n_lat, n_lon = sizes
    count = n_lat // 2 * n_lon
    rows = D // 2 // count
    tokens, heads_dev = y.shape[1:]
    friends = sum(size.bit_length() - 1 for size in sizes)
    dma = pltpu.SemaphoreType.DMA
    vmem = pl.BlockSpec(memory_space=pltpu.VMEM)
    hbm = pl.BlockSpec(memory_space=pl.ANY)
    low, wide = jnp.bfloat16, jnp.float32
    return pl.pallas_call(
        functools.partial(grads_kernel, sizes),
        out_shape=(
            jax.ShapeDtypeStruct((3, D, heads_dev), low),
            jax.ShapeDtypeStruct((heads_dev, D), low),
            jax.ShapeDtypeStruct((replicas - 1, 4, PAIR, D), low),
            jax.ShapeDtypeStruct((4, PAIR, D), low),
            jax.ShapeDtypeStruct((D // 128, 128), wide),
        ),
        in_specs=[vmem, vmem, vmem, vmem, hbm],
        out_specs=(hbm, hbm, hbm, hbm, vmem),
        scratch_shapes=[
            pltpu.VMEM((tokens, D // 2), low),
            pltpu.VMEM((tokens, D // 2), low),
            pltpu.VMEM((4, tokens, heads_dev), low),
            pltpu.VMEM((3, rows, heads_dev), low),
            pltpu.VMEM((heads_dev, rows), low),
            pltpu.VMEM((count - 1, 3, rows, heads_dev), low),
            pltpu.VMEM((count - 1, heads_dev, rows), low),
            pltpu.VMEM((3, rows, heads_dev), wide),
            pltpu.VMEM((heads_dev, rows), wide),
            pltpu.VMEM((friends + 1, D // 128, 128), wide),
            pltpu.VMEM((friends, D // 128, 128), wide),
            pltpu.VMEM((4, PAIR, D), low),
            pltpu.VMEM((4, PAIR, D), wide),
            pltpu.VMEM((4, PAIR, D), low),
            dma((3,)),
            dma((3,)),
            dma((count - 1, 4)),
            dma((count - 1, 4)),
            dma((count - 1, 4)),
            dma((count - 1, 4)),
            dma((count, 4)),
            dma((count, 4)),
            dma((replicas - 1,)),
            dma((replicas - 1,)),
            dma((3,)),
            dma((3,)),
            dma((friends,)),
            dma((friends,)),
            dma((7,)),
        ],
        compiler_params=pltpu.CompilerParams(
            collective_id=2, has_side_effects=True, vmem_limit_bytes=60 * 1024 * 1024
        ),
    )(x, c, y, gain, back)


def attention_kernel(
    group,
    blocked_ref,
    x_ref,
    c_ref,
    w_ref,
    out_w_ref,
    gain_ref,
    y_ref,
    branch_ref,
    rolled_ref,
    gain_out,
    q_low,
    k_low,
    v_low,
    d_low,
    branch_acc,
    rolled_acc,
):
    window_size = 4 * QUARTER
    step = pl.program_id(1)
    scale = HEAD ** (-0.5)
    width = w_ref.shape[2]
    x, c = x_ref[...], c_ref[...]
    for index, target in enumerate((q_low, k_low, v_low)):
        target[...] = jnp.dot(x, w_ref[index], preferred_element_type=jnp.float32).astype(
            jnp.bfloat16
        )
    d_low[...] = contract_cols(c, out_w_ref[...]).astype(jnp.bfloat16)
    lane = lax.broadcasted_iota(jnp.int32, (window_size, 128), 1)
    lower = lane < HEAD
    contract = (((0,), (0,)), ((), ()))
    for window in range(group):
        blocked = blocked_ref[window] < 0
        at = slice(window * window_size, (window + 1) * window_size)
        for pair in range(width // 128):
            cols = slice(pair * 128, (pair + 1) * 128)
            q, k, v, d = q_low[at, cols], k_low[at, cols], v_low[at, cols], d_low[at, cols]
            results = []
            for head in range(2):
                mine = lower if head == 0 else jnp.logical_not(lower)
                q_head = jnp.where(mine, q, jnp.zeros_like(q))
                d_head = jnp.where(mine, d, jnp.zeros_like(d))
                scores = jnp.where(blocked, -1e30, contract_cols(q_head, k) * scale)
                exponent = jnp.exp(scores - jnp.max(scores, -1, keepdims=True))
                weights = exponent / jnp.sum(exponent, -1, keepdims=True)
                weights_low = weights.astype(jnp.bfloat16)
                d_weights = contract_cols(d_head, v)
                row_dots = jnp.sum(weights * d_weights, -1, keepdims=True)
                d_scores = (weights * (d_weights - row_dots) * scale).astype(jnp.bfloat16)
                results.append(
                    (
                        jnp.dot(d_scores, k, preferred_element_type=jnp.float32),
                        lax.dot_general(
                            d_scores, q, contract, preferred_element_type=jnp.float32
                        ),
                        lax.dot_general(
                            weights_low, d, contract, preferred_element_type=jnp.float32
                        ),
                        jnp.dot(weights_low, v, preferred_element_type=jnp.float32),
                    )
                )
            for index in range(4):
                y_ref[index, at, cols] = jnp.where(
                    lower, results[0][index], results[1][index]
                ).astype(jnp.bfloat16)

    branch = jnp.dot(y_ref[3], out_w_ref[...], preferred_element_type=jnp.float32)
    rolled = contract_cols(y_ref[0], w_ref[0])
    rolled += contract_cols(y_ref[1], w_ref[1])
    rolled += contract_cols(y_ref[2], w_ref[2])

    @pl.when(step == 0)
    def _():
        branch_acc[...] = branch
        rolled_acc[...] = rolled

    @pl.when(step > 0)
    def _():
        branch_acc[...] += branch
        rolled_acc[...] += rolled

    @pl.when(step == pl.num_programs(1) - 1)
    def _():
        branch_ref[...] = branch_acc[...].astype(jnp.bfloat16)
        low = rolled_acc[...].astype(jnp.bfloat16)
        rolled_ref[...] = low
        product = low.astype(jnp.float32) * x_ref[...].astype(jnp.float32)
        gain_out[0] = jnp.sum(product, 0, keepdims=True) / gain_ref[...]


def attention(x, c, w_three, w_out, gain, blocked):
    total = x.shape[0]
    heads_dev = w_three.shape[2]
    width = min(256, heads_dev)
    window_size = 4 * QUARTER
    group = 2
    tile = group * window_size
    low, wide = jnp.bfloat16, jnp.float32
    return pl.pallas_call(
        functools.partial(attention_kernel, group),
        grid=(total // tile, heads_dev // width),
        in_specs=[
            pl.BlockSpec((group, window_size, window_size), lambda g, j: (g, 0, 0)),
            pl.BlockSpec((tile, D), lambda g, j: (g, 0)),
            pl.BlockSpec((tile, D), lambda g, j: (g, 0)),
            pl.BlockSpec((3, D, width), lambda g, j: (0, 0, j)),
            pl.BlockSpec((width, D), lambda g, j: (j, 0)),
            pl.BlockSpec((1, D), lambda g, j: (0, 0)),
        ],
        out_specs=(
            pl.BlockSpec((4, tile, width), lambda g, j: (0, g, j)),
            pl.BlockSpec((tile, D), lambda g, j: (g, 0)),
            pl.BlockSpec((tile, D), lambda g, j: (g, 0)),
            pl.BlockSpec((1, 1, D), lambda g, j: (g, 0, 0)),
        ),
        out_shape=(
            jax.ShapeDtypeStruct((4, total, heads_dev), low),
            jax.ShapeDtypeStruct((total, D), low),
            jax.ShapeDtypeStruct((total, D), low),
            jax.ShapeDtypeStruct((total // tile, 1, D), wide),
        ),
        scratch_shapes=[pltpu.VMEM((tile, width), low)] * 4 + [pltpu.VMEM((tile, D), wide)] * 2,
        compiler_params=pltpu.CompilerParams(
            dimension_semantics=("arbitrary", "arbitrary"), vmem_limit_bytes=48 * 1024 * 1024
        ),
    )(blocked, x, c, w_three, w_out, gain.reshape(1, D))


def normalize(tokens):
    values_f = tokens.astype(jnp.float32)
    average = jnp.mean(values_f, -1, keepdims=True)
    centered = values_f - average
    inverse_std = lax.rsqrt(jnp.mean(centered * centered, -1, keepdims=True) + epsilon)
    return (centered * inverse_std, inverse_std)


def contract_cols(left, right):
    return lax.dot_general(
        left, right, (((1,), (1,)), ((), ())), preferred_element_type=jnp.float32
    )


def to_blocks(tensor):
    shaped = tensor.reshape(2, CLAT, 2, WLON // 2, LEV, D)
    blocks = [shaped[1 - a, :, 1 - b].reshape(QUARTER, D) for a in range(2) for b in range(2)]
    return jnp.stack(blocks)


def from_blocks(blocks):
    shaped = blocks.reshape(2, 2, CLAT, WLON // 2, LEV, D)
    rows = [jnp.concatenate([shaped[a, 1], shaped[a, 0]], axis=1) for a in (1, 0)]
    return jnp.concatenate(rows, axis=0)


def shards(tokens, norm_gain, w_qkv, w_out, grad_out):
    sizes = tuple(lax.axis_size(name) for name in ("outer", "lat", "lon"))
    replicas, lat_count, lon_count = sizes
    assert tokens.shape[:3] == (2 * CLAT, LEV, WLON)
    lat_index = lax.axis_index("lat")
    window_size = 4 * QUARTER
    total = replicas * window_size
    w_three = w_qkv.transpose(1, 0, 2)
    tokens_n = tokens.transpose(0, 2, 1, 3)
    grad_n = grad_out.transpose(0, 2, 1, 3)
    standard, inverse_std = normalize(tokens_n)
    normed = (standard * norm_gain).astype(jnp.bfloat16)
    filler = jnp.zeros((4, PAIR - 2 * QUARTER, D), jnp.bfloat16)
    sent = jnp.concatenate([to_blocks(normed), to_blocks(grad_n), filler], axis=1)
    arrived = front_exchange(sizes, sent)
    gathered = arrived[:, :, :QUARTER].reshape(total, D)
    cot_all = arrived[:, :, QUARTER : 2 * QUARTER].reshape(total, D)

    cut_window = jnp.logical_and(lat_index == lat_count - 1, jnp.arange(replicas) == replicas - 1)
    half_index = jnp.arange(window_size) // (2 * QUARTER)
    other_half = half_index[:, None] != half_index[None, :]
    blocked = jnp.where(jnp.logical_and(cut_window[:, None, None], other_half[None]), -1.0, 0.0)
    y, branch, d_rolled, gain_local = attention(
        gathered, cot_all, w_three, w_out, norm_gain, blocked.astype(jnp.float32)
    )
    gain_local = jnp.sum(gain_local, (0, 1))
    in_blocks = (replicas, 4, QUARTER, D)
    back = jnp.concatenate(
        [
            branch.reshape(in_blocks),
            d_rolled.reshape(in_blocks),
            jnp.zeros((replicas, 4, PAIR - 2 * QUARTER, D), jnp.bfloat16),
        ],
        axis=2,
    )
    grad_qkv, grad_out_w, _, summed, grad_gain = grads_exchange(
        sizes, gathered, cot_all, y, gain_local.reshape(D // 128, 128), back
    )
    branch_low = from_blocks(summed[:, :QUARTER])
    d_normed = from_blocks(summed[:, QUARTER : 2 * QUARTER]).astype(jnp.float32)
    output = (tokens_n.astype(jnp.float32) + branch_low.astype(jnp.float32)).astype(jnp.bfloat16)
    scaled = d_normed * norm_gain
    d_local = inverse_std * (
        scaled
        - jnp.mean(scaled, -1, keepdims=True)
        - standard * jnp.mean(scaled * standard, -1, keepdims=True)
    )
    grad_tokens = (grad_n.astype(jnp.float32) + d_local).astype(jnp.bfloat16)
    grad_wqkv = grad_qkv.astype(jnp.float32).transpose(1, 0, 2)
    grad_wout = grad_out_w.astype(jnp.float32)
    return (
        output.transpose(0, 2, 1, 3),
        grad_tokens.transpose(0, 2, 1, 3),
        grad_wqkv,
        grad_wout,
        grad_gain.reshape(D),
    )


def solution(mesh):
    in_specs = (
        P(("outer", "lat"), None, "lon", None),
        P(),
        P(None, None, "outer"),
        P("outer", None),
        P(("outer", "lat"), None, "lon", None),
    )
    out_specs = (
        P(("outer", "lat"), None, "lon", None),
        P(("outer", "lat"), None, "lon", None),
        P(None, None, "outer"),
        P("outer", None),
        P(),
    )
    return jax.shard_map(shards, mesh=mesh, in_specs=in_specs, out_specs=out_specs, check_vma=False)
```

```python
import functools

import jax
import jax.numpy as jnp
from jax import lax
from jax.experimental import pallas as pl
from jax.experimental.pallas import tpu as pltpu
from jax.sharding import PartitionSpec as P

D = 2048
HEAD = 64
LEV = 2
CLAT = 3
WLON = 12
QUARTER = CLAT * LEV * WLON // 2
PART = 40
PAIR = 2 * PART
TILE = 4 * PART
MESH = pl.DeviceIdType.MESH
epsilon = 1e-05


def position():
    return lax.axis_index("outer"), lax.axis_index("lat"), lax.axis_index("lon")


def enter(receivers, senders):
    barrier = pltpu.get_barrier_semaphore()
    for device in senders:
        pl.semaphore_signal(barrier, inc=1, device_id=device, device_id_type=MESH)
    pl.semaphore_wait(barrier, len(receivers))


def shifted(sizes, band, lat, lon, rows, columns):
    replicas, n_lat, n_lon = sizes
    flat = lax.rem(band * n_lat + lat + rows + replicas * n_lat, replicas * n_lat)
    return flat // n_lat, lax.rem(flat, n_lat), lax.rem(lon + columns + n_lon, n_lon)


def gather_routes(sizes):
    outer, lat, lon = position()
    routes = []
    for step in range(sizes[0]):
        for a in range(2):
            for b in range(2):
                band, lat_to, lon_to = shifted(sizes, outer, lat, lon, -a, -b)
                group = lax.rem(band + step, sizes[0])
                band_from, lat_from, lon_from = shifted(sizes, outer, lat, lon, a, b)
                tile_from = lax.rem(outer - step + sizes[0], sizes[0])
                source_band, source_lat, source_lon = shifted(sizes, tile_from, lat, lon, a, b)
                routes.append(
                    (
                        step,
                        2 * a + b,
                        (group, lat_to, lon_to),
                        band,
                        (source_band, source_lat, source_lon),
                        tile_from,
                    )
                )
    return routes


def standardize(values):
    centered = values - jnp.mean(values, -1, keepdims=True)
    inverse_std = lax.rsqrt(jnp.mean(centered * centered, -1, keepdims=True) + epsilon)
    return centered * inverse_std, inverse_std


def front_kernel(sizes, token_ref, grad_ref, gain_ref, got, src, send_sem, recv_sem, local_sem):
    for block in range(4):
        standard, _ = standardize(token_ref[block].astype(jnp.float32))
        both = [standard * gain_ref[...], grad_ref[block].astype(jnp.float32)]
        src[block] = jnp.concatenate(both, axis=0).astype(jnp.bfloat16)
    routes = gather_routes(sizes)
    remote = [r for r in routes if (r[0], r[1]) != (0, 0)]
    remote = [r for r in remote if r[0] > 0] + [r for r in remote if r[0] == 0]
    enter([r[2] for r in remote], [r[4] for r in remote])
    outer, _, _ = position()
    copies = []
    for index, (step, block, target, tile, _, tile_from) in enumerate(remote):
        push = pltpu.make_async_remote_copy(
            src.at[block],
            got.at[tile, block],
            send_sem.at[index],
            recv_sem.at[index],
            device_id=target,
            device_id_type=MESH,
        )
        push.start()
        arrive = pltpu.make_async_remote_copy(
            src.at[block],
            got.at[tile_from, block],
            send_sem.at[index],
            recv_sem.at[index],
            device_id=target,
            device_id_type=MESH,
        )
        copies.append((push, arrive))
    own = pltpu.make_async_copy(src.at[0], got.at[outer, 0], local_sem)
    own.start()
    for push, arrive in copies:
        arrive.wait_recv()
    for push, arrive in copies:
        push.wait_send()
    own.wait()


def front_exchange(sizes, token_blocks, grad_blocks, gain):
    replicas = sizes[0]
    count = 4 * replicas - 1
    return pl.pallas_call(
        functools.partial(front_kernel, sizes),
        out_shape=jax.ShapeDtypeStruct((replicas, 4, PAIR, D), jnp.bfloat16),
        in_specs=[pl.BlockSpec(memory_space=pltpu.VMEM)] * 3,
        out_specs=pl.BlockSpec(memory_space=pl.ANY),
        scratch_shapes=[
            pltpu.VMEM((4, PAIR, D), jnp.bfloat16),
            pltpu.SemaphoreType.DMA((count,)),
            pltpu.SemaphoreType.DMA((count,)),
            pltpu.SemaphoreType.DMA(()),
        ],
        compiler_params=pltpu.CompilerParams(
            collective_id=1, has_side_effects=True, vmem_limit_bytes=32 * 1024 * 1024
        ),
    )(token_blocks, grad_blocks, gain)


def xor_partners(sizes):
    outer, lat, lon = position()
    result = []
    for axis, size in enumerate(sizes):
        bit = 1
        while bit < size:
            at = [outer, lat, lon]
            lower = lax.rem(at[axis] // bit, 2)
            at[axis] = at[axis] + bit * (1 - 2 * lower)
            result.append(tuple(at))
            bit *= 2
    return result


def grads_kernel(
    sizes,
    x_ref,
    c_ref,
    y_ref,
    gain_ref,
    token_ref,
    grad_ref,
    norm_ref,
    back_ref,
    qkv_ref,
    out_ref,
    shares_ref,
    gain_out,
    output_ref,
    d_tokens_ref,
    x_pair,
    c_pair,
    y_pair,
    first_q,
    first_o,
    slots_q,
    slots_o,
    own_q,
    own_o,
    gain_acc,
    gain_slots,
    tile_in,
    tile_sum,
    tile_low,
    got_ref,
    pair_send,
    pair_recv,
    rs_send,
    rs_recv,
    ag_send,
    ag_recv,
    share_send,
    share_recv,
    outer_send,
    outer_recv,
    back_send,
    back_recv,
    gain_send,
    gain_recv,
    local_sem,
):
    replicas, n_lat, n_lon = sizes
    outer, lat, lon = position()
    count = n_lat // 2 * n_lon
    rows = D // 2 // count
    half = lax.rem(lat, 2)
    upper = lat // 2
    partner = (outer, lat + 1 - 2 * half, lon)

    def on_ring(place):
        place = lax.rem(place + count, count)
        turned = jnp.where(half == 0, place, count - 1 - place)
        row = turned // n_lon
        column = lax.rem(turned, n_lon)
        return (outer, 2 * row + half, jnp.where(lax.rem(row, 2) == 0, column, n_lon - 1 - column))

    along = jnp.where(lax.rem(upper, 2) == 0, lon, n_lon - 1 - lon)
    spot = upper * n_lon + along
    me = jnp.where(half == 0, spot, count - 1 - spot)
    after, before = on_ring(me + 1), on_ring(me - 1)

    groups_to = [(lax.rem(outer + step, replicas), lat, lon) for step in range(1, replicas)]
    groups_from = [
        (lax.rem(outer - step + replicas, replicas), lat, lon) for step in range(1, replicas)
    ]
    moves = [(0, 1), (1, 0), (1, 1)]
    halo_to = [shifted(sizes, outer, lat, lon, a, b) for a, b in moves]
    halo_from = [shifted(sizes, outer, lat, lon, -a, -b) for a, b in moves]
    friends = xor_partners(sizes)
    enter(
        [after, partner] + groups_to + halo_to + friends,
        [before, partner] + groups_from + halo_from + friends,
    )

    def remote(src, dst, send, recv, device):
        return pltpu.make_async_remote_copy(
            src, dst, send, recv, device_id=device, device_id_type=MESH
        )

    half_d = D // 2
    theirs = pl.ds(pl.multiple_of((1 - half) * half_d, half_d), half_d)
    swaps = [
        remote(x_ref.at[:, theirs], x_pair, pair_send.at[0], pair_recv.at[0], partner),
        remote(y_ref, y_pair, pair_send.at[1], pair_recv.at[1], partner),
        remote(c_ref.at[:, theirs], c_pair, pair_send.at[2], pair_recv.at[2], partner),
    ]
    for swap in swaps:
        swap.start()
    back = []
    for index, target in enumerate(groups_to):
        push = remote(
            back_ref.at[target[0]],
            shares_ref.at[index],
            outer_send.at[index],
            outer_recv.at[index],
            target,
        )
        push.start()
        back.append(push)
    for swap in swaps:
        swap.wait_recv()

    contract = (((0,), (0,)), ((), ()))

    def product(chunk, part):
        here = pl.ds(pl.multiple_of(half * half_d + chunk * rows, rows), rows)
        there = pl.ds(pl.multiple_of(chunk * rows, rows), rows)
        if part < 3:
            pairs = [(x_ref[:, here], y_ref[part]), (x_pair[:, there], y_pair[part])]
        else:
            pairs = [(y_ref[3], c_ref[:, here]), (y_pair[3], c_pair[:, there])]
        mine, other = [
            lax.dot_general(left, right, contract, preferred_element_type=jnp.float32)
            for left, right in pairs
        ]
        return mine + other

    def first_at(part):
        return first_q.at[part] if part < 3 else first_o

    def own_at(part):
        return own_q.at[part] if part < 3 else own_o

    def slot_at(step, part):
        return slots_q.at[step, part] if part < 3 else slots_o.at[step]

    def ring_copy(src, step, part):
        return remote(
            src, slot_at(step, part), rs_send.at[step, part], rs_recv.at[step, part], after
        )

    for part in range(4):
        first_at(part)[...] = product(me, part).astype(jnp.bfloat16)
        ring_copy(first_at(part), 0, part).start()

    def reduce_step(step, carry):
        chunk = lax.rem(me - step - 1 + count, count)
        for part in range(4):
            own_at(part)[...] = product(chunk, part)
        for part in range(4):
            slot = slot_at(step, part)
            ring_copy(first_at(part), step, part).wait_recv()
            slot[...] = (slot[...].astype(jnp.float32) + own_at(part)[...]).astype(jnp.bfloat16)

            @pl.when(step < count - 2)
            def _():
                ring_copy(slot_at(step, part), step + 1, part).start()

        return carry

    lax.fori_loop(0, count - 1, reduce_step, 0)

    def place(side, chunk, part):
        start = pl.multiple_of(side * half_d + chunk * rows, rows)
        if part < 3:
            return qkv_ref.at[part, pl.ds(start, rows)]
        return out_ref.at[:, pl.ds(start, rows)]

    done = lax.rem(me + 1, count)
    pending = []
    for part in range(4):
        final = slot_at(count - 2, part)
        target = place(half, done, part)
        spread = remote(final, target, ag_send.at[0, part], ag_recv.at[0, part], after)
        spread.start()
        share = remote(final, target, share_send.at[0, part], share_recv.at[0, part], partner)
        share.start()
        store = pltpu.make_async_copy(final, target, local_sem.at[part])
        store.start()
        pending.append((spread, share, store))

    def gain_copy(step):
        return remote(
            gain_acc.at[step],
            gain_slots.at[step],
            gain_send.at[step],
            gain_recv.at[step],
            friends[step],
        )

    gain_acc[0] = gain_ref[...]
    gain_copy(0).start()
    rounds = len(friends)

    def gain_round(step):
        gain_copy(step).wait_recv()
        gain_acc[step + 1] = gain_acc[step] + gain_slots[step]
        if step + 1 < rounds:
            gain_copy(step + 1).start()

    load = pltpu.make_async_copy(back_ref.at[outer], tile_in, local_sem.at[4])
    load.start()
    load.wait()
    tile_sum[...] = tile_in[...].astype(jnp.float32)
    for index in range(replicas - 1):
        back[index].wait_recv()
        load = pltpu.make_async_copy(shares_ref.at[index], tile_in, local_sem.at[5])
        load.start()
        load.wait()
        tile_sum[...] += tile_in[...].astype(jnp.float32)
    tile_low[...] = tile_sum[...].astype(jnp.bfloat16)
    keep = pltpu.make_async_copy(tile_low.at[0], got_ref.at[0], local_sem.at[6])
    keep.start()
    halos = []
    for index, (a, b) in enumerate(moves):
        block = 2 * a + b
        push = remote(
            tile_low.at[block],
            got_ref.at[block],
            back_send.at[index],
            back_recv.at[index],
            halo_to[index],
        )
        push.start()
        halos.append(push)

    def finish(block):
        if block == 0:
            keep.wait()
        else:
            halos[block - 1].wait_recv()
        back_values = got_ref[block].astype(jnp.float32)
        values = token_ref[block].astype(jnp.float32)
        standard, inverse_std = standardize(values)
        output_ref[block] = (values + back_values[:PART]).astype(jnp.bfloat16)
        scaled = back_values[PART:] * norm_ref[...]
        d_local = inverse_std * (
            scaled
            - jnp.mean(scaled, -1, keepdims=True)
            - standard * jnp.mean(scaled * standard, -1, keepdims=True)
        )
        d_tokens_ref[block] = (grad_ref[block].astype(jnp.float32) + d_local).astype(jnp.bfloat16)

    sends = []
    for step in range(count - 1):
        chunk = lax.rem(me - step + count, count)
        for part in range(4):
            here = place(half, chunk, part)
            remote(
                slot_at(count - 2, part), here, ag_send.at[step, part], ag_recv.at[step, part], after
            ).wait_recv()
            if step < count - 2:
                spread = remote(
                    here, here, ag_send.at[step + 1, part], ag_recv.at[step + 1, part], after
                )
                spread.start()
                sends.append(spread)
            share = remote(
                here, here, share_send.at[step + 1, part], share_recv.at[step + 1, part], partner
            )
            share.start()
            sends.append(share)
        if step < rounds:
            gain_round(step)
        if 3 <= step < 7:
            finish(step - 3)
    for step in range(count - 1, rounds):
        gain_round(step)
    gain_out[...] = gain_acc[rounds]

    partner_me = jnp.where(half == 0, count - 1 - spot, spot)
    for step in range(count):
        chunk = lax.rem(partner_me + 1 - step + count, count)
        for part in range(4):
            remote(
                slot_at(count - 2, part),
                place(1 - half, chunk, part),
                share_send.at[step, part],
                share_recv.at[step, part],
                partner,
            ).wait_recv()
    for push in halos:
        push.wait_send()
    for push in back:
        push.wait_send()
    for swap in swaps:
        swap.wait_send()
    for part in range(4):
        ring_copy(first_at(part), 0, part).wait_send()

    def drain(step, carry):
        for part in range(4):
            ring_copy(slot_at(step, part), step + 1, part).wait_send()
        return carry

    lax.fori_loop(0, count - 2, drain, 0)
    for spread, share, store in pending:
        spread.wait_send()
        share.wait_send()
        store.wait()
    for copy in sends:
        copy.wait_send()
    for step in range(rounds):
        gain_copy(step).wait_send()


def grads_exchange(sizes, x, c, y, gain, token_blocks, grad_blocks, norm_gain, back):
    replicas, n_lat, n_lon = sizes
    count = n_lat // 2 * n_lon
    rows = D // 2 // count
    tokens, heads_dev = y.shape[1:]
    friends = sum(size.bit_length() - 1 for size in sizes)
    dma = pltpu.SemaphoreType.DMA
    vmem = pl.BlockSpec(memory_space=pltpu.VMEM)
    hbm = pl.BlockSpec(memory_space=pl.ANY)
    low, wide = jnp.bfloat16, jnp.float32
    return pl.pallas_call(
        functools.partial(grads_kernel, sizes),
        out_shape=(
            jax.ShapeDtypeStruct((3, D, heads_dev), low),
            jax.ShapeDtypeStruct((heads_dev, D), low),
            jax.ShapeDtypeStruct((replicas - 1, 4, PAIR, D), low),
            jax.ShapeDtypeStruct((D // 128, 128), wide),
            jax.ShapeDtypeStruct((4, PART, D), low),
            jax.ShapeDtypeStruct((4, PART, D), low),
        ),
        in_specs=[vmem] * 7 + [hbm],
        out_specs=(hbm, hbm, hbm, vmem, vmem, vmem),
        scratch_shapes=[
            pltpu.VMEM((tokens, D // 2), low),
            pltpu.VMEM((tokens, D // 2), low),
            pltpu.VMEM((4, tokens, heads_dev), low),
            pltpu.VMEM((3, rows, heads_dev), low),
            pltpu.VMEM((heads_dev, rows), low),
            pltpu.VMEM((count - 1, 3, rows, heads_dev), low),
            pltpu.VMEM((count - 1, heads_dev, rows), low),
            pltpu.VMEM((3, rows, heads_dev), wide),
            pltpu.VMEM((heads_dev, rows), wide),
            pltpu.VMEM((friends + 1, D // 128, 128), wide),
            pltpu.VMEM((friends, D // 128, 128), wide),
            pltpu.VMEM((4, PAIR, D), low),
            pltpu.VMEM((4, PAIR, D), wide),
            pltpu.VMEM((4, PAIR, D), low),
            pltpu.VMEM((4, PAIR, D), low),
            dma((3,)),
            dma((3,)),
            dma((count - 1, 4)),
            dma((count - 1, 4)),
            dma((count - 1, 4)),
            dma((count - 1, 4)),
            dma((count, 4)),
            dma((count, 4)),
            dma((replicas - 1,)),
            dma((replicas - 1,)),
            dma((3,)),
            dma((3,)),
            dma((friends,)),
            dma((friends,)),
            dma((7,)),
        ],
        compiler_params=pltpu.CompilerParams(
            collective_id=2, has_side_effects=True, vmem_limit_bytes=60 * 1024 * 1024
        ),
    )(x, c, y, gain, token_blocks, grad_blocks, norm_gain, back)


def attention_kernel(
    group,
    blocked_ref,
    arrived_ref,
    w_ref,
    out_w_ref,
    gain_ref,
    y_ref,
    x_ref,
    c_ref,
    back_ref,
    gain_out,
    q_low,
    k_low,
    v_low,
    d_low,
    branch_acc,
    rolled_acc,
):
    step = pl.program_id(1)

    @pl.when(step == 0)
    def _():
        for window in range(group):
            parts = [arrived_ref[window, block].astype(jnp.float32) for block in range(4)]
            at = slice(window * TILE, (window + 1) * TILE)
            x_ref[at] = jnp.concatenate([part[:PART] for part in parts], 0).astype(jnp.bfloat16)
            c_ref[at] = jnp.concatenate([part[PART:] for part in parts], 0).astype(jnp.bfloat16)

    scale = HEAD ** (-0.5)
    width = w_ref.shape[2]
    x, c = x_ref[...], c_ref[...]
    for index, target in enumerate((q_low, k_low, v_low)):
        target[...] = jnp.dot(x, w_ref[index], preferred_element_type=jnp.float32).astype(
            jnp.bfloat16
        )
    d_low[...] = contract_cols(c, out_w_ref[...]).astype(jnp.bfloat16)
    lane = lax.broadcasted_iota(jnp.int32, (TILE, 128), 1)
    lower = lane < HEAD
    contract = (((0,), (0,)), ((), ()))
    for window in range(group):
        blocked = blocked_ref[window] < 0
        at = slice(window * TILE, (window + 1) * TILE)
        for pair in range(width // 128):
            cols = slice(pair * 128, (pair + 1) * 128)
            q, k, v, d = q_low[at, cols], k_low[at, cols], v_low[at, cols], d_low[at, cols]
            results = []
            for head in range(2):
                mine = lower if head == 0 else jnp.logical_not(lower)
                q_head = jnp.where(mine, q, jnp.zeros_like(q))
                d_head = jnp.where(mine, d, jnp.zeros_like(d))
                scores = jnp.where(blocked, -1e30, contract_cols(q_head, k) * scale)
                exponent = jnp.exp(scores - jnp.max(scores, -1, keepdims=True))
                weights = exponent / jnp.sum(exponent, -1, keepdims=True)
                weights_low = weights.astype(jnp.bfloat16)
                d_weights = contract_cols(d_head, v)
                row_dots = jnp.sum(weights * d_weights, -1, keepdims=True)
                d_scores = (weights * (d_weights - row_dots) * scale).astype(jnp.bfloat16)
                results.append(
                    (
                        jnp.dot(d_scores, k, preferred_element_type=jnp.float32),
                        lax.dot_general(
                            d_scores, q, contract, preferred_element_type=jnp.float32
                        ),
                        lax.dot_general(
                            weights_low, d, contract, preferred_element_type=jnp.float32
                        ),
                        jnp.dot(weights_low, v, preferred_element_type=jnp.float32),
                    )
                )
            for index in range(4):
                y_ref[index, at, cols] = jnp.where(
                    lower, results[0][index], results[1][index]
                ).astype(jnp.bfloat16)

    branch = jnp.dot(y_ref[3], out_w_ref[...], preferred_element_type=jnp.float32)
    rolled = contract_cols(y_ref[0], w_ref[0])
    rolled += contract_cols(y_ref[1], w_ref[1])
    rolled += contract_cols(y_ref[2], w_ref[2])

    @pl.when(step == 0)
    def _():
        branch_acc[...] = branch
        rolled_acc[...] = rolled

    @pl.when(step > 0)
    def _():
        branch_acc[...] += branch
        rolled_acc[...] += rolled

    @pl.when(step == pl.num_programs(1) - 1)
    def _():
        for window in range(group):
            for block in range(4):
                start = window * TILE + block * PART
                at = slice(start, start + PART)
                both = jnp.concatenate([branch_acc[at], rolled_acc[at]], axis=0)
                back_ref[window, block] = both.astype(jnp.bfloat16)
        low = rolled_acc[...].astype(jnp.bfloat16)
        product = low.astype(jnp.float32) * x_ref[...].astype(jnp.float32)
        gain_out[0] = jnp.sum(product, 0, keepdims=True) / gain_ref[...]


def attention(arrived, w_three, w_out, gain, blocked):
    replicas = arrived.shape[0]
    total = replicas * TILE
    heads_dev = w_three.shape[2]
    width = min(256, heads_dev)
    group = 2
    tile = group * TILE
    low, wide = jnp.bfloat16, jnp.float32
    return pl.pallas_call(
        functools.partial(attention_kernel, group),
        grid=(total // tile, heads_dev // width),
        in_specs=[
            pl.BlockSpec((group, TILE, TILE), lambda g, j: (g, 0, 0)),
            pl.BlockSpec((group, 4, PAIR, D), lambda g, j: (g, 0, 0, 0)),
            pl.BlockSpec((3, D, width), lambda g, j: (0, 0, j)),
            pl.BlockSpec((width, D), lambda g, j: (j, 0)),
            pl.BlockSpec((1, D), lambda g, j: (0, 0)),
        ],
        out_specs=(
            pl.BlockSpec((4, tile, width), lambda g, j: (0, g, j)),
            pl.BlockSpec((tile, D), lambda g, j: (g, 0)),
            pl.BlockSpec((tile, D), lambda g, j: (g, 0)),
            pl.BlockSpec((group, 4, PAIR, D), lambda g, j: (g, 0, 0, 0)),
            pl.BlockSpec((1, 1, D), lambda g, j: (g, 0, 0)),
        ),
        out_shape=(
            jax.ShapeDtypeStruct((4, total, heads_dev), low),
            jax.ShapeDtypeStruct((total, D), low),
            jax.ShapeDtypeStruct((total, D), low),
            jax.ShapeDtypeStruct((replicas, 4, PAIR, D), low),
            jax.ShapeDtypeStruct((total // tile, 1, D), wide),
        ),
        scratch_shapes=[pltpu.VMEM((tile, width), low)] * 4 + [pltpu.VMEM((tile, D), wide)] * 2,
        compiler_params=pltpu.CompilerParams(
            dimension_semantics=("arbitrary", "arbitrary"), vmem_limit_bytes=48 * 1024 * 1024
        ),
    )(blocked, arrived, w_three, w_out, gain)


def contract_cols(left, right):
    return lax.dot_general(
        left, right, (((1,), (1,)), ((), ())), preferred_element_type=jnp.float32
    )


def to_blocks(tensor):
    shaped = tensor.reshape(2, CLAT, 2, WLON // 2, LEV, D)
    blocks = [shaped[1 - a, :, 1 - b].reshape(QUARTER, D) for a in range(2) for b in range(2)]
    return jnp.pad(jnp.stack(blocks), ((0, 0), (0, PART - QUARTER), (0, 0)))


def from_blocks(blocks):
    shaped = blocks[:, :QUARTER].reshape(2, 2, CLAT, WLON // 2, LEV, D)
    rows = [jnp.concatenate([shaped[a, 1], shaped[a, 0]], axis=1) for a in (1, 0)]
    return jnp.concatenate(rows, axis=0)


def shards(tokens, norm_gain, w_qkv, w_out, grad_out):
    sizes = tuple(lax.axis_size(name) for name in ("outer", "lat", "lon"))
    replicas, lat_count, lon_count = sizes
    assert tokens.shape[:3] == (2 * CLAT, LEV, WLON)
    lat_index = lax.axis_index("lat")
    w_three = w_qkv.transpose(1, 0, 2)
    gain = norm_gain.reshape(1, D)
    token_blocks = to_blocks(tokens.transpose(0, 2, 1, 3))
    grad_blocks = to_blocks(grad_out.transpose(0, 2, 1, 3))
    arrived = front_exchange(sizes, token_blocks, grad_blocks, gain)
    cut_window = jnp.logical_and(lat_index == lat_count - 1, jnp.arange(replicas) == replicas - 1)
    spot = jnp.arange(TILE)
    half_index = spot // (2 * PART)
    other_half = half_index[:, None] != half_index[None, :]
    blocked = jnp.logical_and(cut_window[:, None, None], other_half[None])
    blocked = jnp.logical_or(blocked, (spot % PART >= QUARTER)[None, None])
    y, x, c, back, gain_local = attention(
        arrived, w_three, w_out, gain, jnp.where(blocked, -1.0, 0.0).astype(jnp.float32)
    )
    gain_local = jnp.sum(gain_local, (0, 1)).reshape(D // 128, 128)
    grad_qkv, grad_out_w, _, grad_gain, output, grad_tokens = grads_exchange(
        sizes, x, c, y, gain_local, token_blocks, grad_blocks, gain, back
    )
    grad_wqkv = grad_qkv.astype(jnp.float32).transpose(1, 0, 2)
    grad_wout = grad_out_w.astype(jnp.float32)
    return (
        from_blocks(output).transpose(0, 2, 1, 3),
        from_blocks(grad_tokens).transpose(0, 2, 1, 3),
        grad_wqkv,
        grad_wout,
        grad_gain.reshape(D),
    )


def solution(mesh):
    in_specs = (
        P(("outer", "lat"), None, "lon", None),
        P(),
        P(None, None, "outer"),
        P("outer", None),
        P(("outer", "lat"), None, "lon", None),
    )
    out_specs = (
        P(("outer", "lat"), None, "lon", None),
        P(("outer", "lat"), None, "lon", None),
        P(None, None, "outer"),
        P("outer", None),
        P(),
    )
    return jax.shard_map(shards, mesh=mesh, in_specs=in_specs, out_specs=out_specs, check_vma=False)
```

```python
import functools

import jax
import jax.numpy as jnp
from jax import lax
from jax.experimental import pallas as pl
from jax.experimental.pallas import tpu as pltpu
from jax.sharding import PartitionSpec as P

D = 2048
HEAD = 64
LEV = 2
CLAT = 3
WLON = 12
QUARTER = CLAT * LEV * WLON // 2
PART = 40
PAIR = 2 * PART
TILE = 4 * PART
MESH = pl.DeviceIdType.MESH
epsilon = 1e-05


def position():
    return lax.axis_index("outer"), lax.axis_index("lat"), lax.axis_index("lon")


def enter(receivers, senders):
    barrier = pltpu.get_barrier_semaphore()
    for device in senders:
        pl.semaphore_signal(barrier, inc=1, device_id=device, device_id_type=MESH)
    pl.semaphore_wait(barrier, len(receivers))


def shifted(sizes, band, lat, lon, rows, columns):
    replicas, n_lat, n_lon = sizes
    flat = lax.rem(band * n_lat + lat + rows + replicas * n_lat, replicas * n_lat)
    return flat // n_lat, lax.rem(flat, n_lat), lax.rem(lon + columns + n_lon, n_lon)


def gather_routes(sizes):
    outer, lat, lon = position()
    routes = []
    for step in range(sizes[0]):
        for a in range(2):
            for b in range(2):
                band, lat_to, lon_to = shifted(sizes, outer, lat, lon, -a, -b)
                group = lax.rem(band + step, sizes[0])
                band_from, lat_from, lon_from = shifted(sizes, outer, lat, lon, a, b)
                tile_from = lax.rem(outer - step + sizes[0], sizes[0])
                source_band, source_lat, source_lon = shifted(sizes, tile_from, lat, lon, a, b)
                routes.append(
                    (
                        step,
                        2 * a + b,
                        (group, lat_to, lon_to),
                        band,
                        (source_band, source_lat, source_lon),
                        tile_from,
                    )
                )
    return routes


def standardize(values):
    centered = values - jnp.mean(values, -1, keepdims=True)
    inverse_std = lax.rsqrt(jnp.mean(centered * centered, -1, keepdims=True) + epsilon)
    return centered * inverse_std, inverse_std


def front_kernel(sizes, token_ref, grad_ref, gain_ref, got, src, send_sem, recv_sem, local_sem):
    for block in range(4):
        standard, _ = standardize(token_ref[block].astype(jnp.float32))
        both = [standard * gain_ref[...], grad_ref[block].astype(jnp.float32)]
        src[block] = jnp.concatenate(both, axis=0).astype(jnp.bfloat16)
    routes = gather_routes(sizes)
    remote = [r for r in routes if (r[0], r[1]) != (0, 0)]
    remote = [r for r in remote if r[0] > 0] + [r for r in remote if r[0] == 0]
    enter([r[2] for r in remote], [r[4] for r in remote])
    outer, _, _ = position()
    copies = []
    for index, (step, block, target, tile, _, tile_from) in enumerate(remote):
        push = pltpu.make_async_remote_copy(
            src.at[block],
            got.at[tile, block],
            send_sem.at[index],
            recv_sem.at[index],
            device_id=target,
            device_id_type=MESH,
        )
        push.start()
        arrive = pltpu.make_async_remote_copy(
            src.at[block],
            got.at[tile_from, block],
            send_sem.at[index],
            recv_sem.at[index],
            device_id=target,
            device_id_type=MESH,
        )
        copies.append((push, arrive))
    own = pltpu.make_async_copy(src.at[0], got.at[outer, 0], local_sem)
    own.start()
    for push, arrive in copies:
        arrive.wait_recv()
    for push, arrive in copies:
        push.wait_send()
    own.wait()


def front_exchange(sizes, token_blocks, grad_blocks, gain):
    replicas = sizes[0]
    count = 4 * replicas - 1
    return pl.pallas_call(
        functools.partial(front_kernel, sizes),
        out_shape=jax.ShapeDtypeStruct((replicas, 4, PAIR, D), jnp.bfloat16),
        in_specs=[pl.BlockSpec(memory_space=pltpu.VMEM)] * 3,
        out_specs=pl.BlockSpec(memory_space=pl.ANY),
        scratch_shapes=[
            pltpu.VMEM((4, PAIR, D), jnp.bfloat16),
            pltpu.SemaphoreType.DMA((count,)),
            pltpu.SemaphoreType.DMA((count,)),
            pltpu.SemaphoreType.DMA(()),
        ],
        compiler_params=pltpu.CompilerParams(
            collective_id=1, has_side_effects=True, vmem_limit_bytes=32 * 1024 * 1024
        ),
    )(token_blocks, grad_blocks, gain)


def xor_partners(sizes):
    outer, lat, lon = position()
    result = []
    for axis, size in enumerate(sizes):
        bit = 1
        while bit < size:
            at = [outer, lat, lon]
            lower = lax.rem(at[axis] // bit, 2)
            at[axis] = at[axis] + bit * (1 - 2 * lower)
            result.append(tuple(at))
            bit *= 2
    return result


def grads_kernel(
    sizes,
    x_ref,
    c_ref,
    y_ref,
    gain_ref,
    token_ref,
    grad_ref,
    norm_ref,
    back_ref,
    qkv_ref,
    out_ref,
    shares_ref,
    gain_out,
    output_ref,
    d_tokens_ref,
    x_pair,
    c_pair,
    y_pair,
    first_q,
    first_o,
    slots_q,
    slots_o,
    own_q,
    own_o,
    gain_acc,
    gain_slots,
    tile_in,
    tile_sum,
    tile_low,
    got_ref,
    pair_send,
    pair_recv,
    rs_send,
    rs_recv,
    ag_send,
    ag_recv,
    share_send,
    share_recv,
    outer_send,
    outer_recv,
    back_send,
    back_recv,
    gain_send,
    gain_recv,
    local_sem,
):
    replicas, n_lat, n_lon = sizes
    outer, lat, lon = position()
    count = n_lat // 2 * n_lon
    rows = D // 2 // count
    half = lax.rem(lat, 2)
    upper = lat // 2
    partner = (outer, lat + 1 - 2 * half, lon)

    def on_ring(place):
        place = lax.rem(place + count, count)
        turned = jnp.where(half == 0, place, count - 1 - place)
        row = turned // n_lon
        column = lax.rem(turned, n_lon)
        return (outer, 2 * row + half, jnp.where(lax.rem(row, 2) == 0, column, n_lon - 1 - column))

    along = jnp.where(lax.rem(upper, 2) == 0, lon, n_lon - 1 - lon)
    spot = upper * n_lon + along
    me = jnp.where(half == 0, spot, count - 1 - spot)
    after, before = on_ring(me + 1), on_ring(me - 1)

    groups_to = [(lax.rem(outer + step, replicas), lat, lon) for step in range(1, replicas)]
    groups_from = [
        (lax.rem(outer - step + replicas, replicas), lat, lon) for step in range(1, replicas)
    ]
    moves = [(0, 1), (1, 0), (1, 1)]
    halo_to = [shifted(sizes, outer, lat, lon, a, b) for a, b in moves]
    halo_from = [shifted(sizes, outer, lat, lon, -a, -b) for a, b in moves]
    friends = xor_partners(sizes)
    enter(
        [after, partner] + groups_to + halo_to + friends,
        [before, partner] + groups_from + halo_from + friends,
    )

    def remote(src, dst, send, recv, device):
        return pltpu.make_async_remote_copy(
            src, dst, send, recv, device_id=device, device_id_type=MESH
        )

    order = (3, 0, 1, 2)
    half_d = D // 2
    theirs = pl.ds(pl.multiple_of((1 - half) * half_d, half_d), half_d)
    swaps = [
        remote(c_ref.at[:, theirs], c_pair, pair_send.at[0], pair_recv.at[0], partner),
        remote(x_ref.at[:, theirs], x_pair, pair_send.at[1], pair_recv.at[1], partner),
    ]
    for index, part in enumerate(order):
        copy = remote(
            y_ref.at[part], y_pair.at[part], pair_send.at[2 + index], pair_recv.at[2 + index], partner
        )
        swaps.append(copy)
    swaps = [swaps[0], swaps[2], swaps[1]] + swaps[3:]
    for swap in swaps:
        swap.start()
    back = []
    for index, target in enumerate(groups_to):
        push = remote(
            back_ref.at[target[0]],
            shares_ref.at[index],
            outer_send.at[index],
            outer_recv.at[index],
            target,
        )
        push.start()
        back.append(push)
    contract = (((0,), (0,)), ((), ()))

    def product(chunk, part):
        here = pl.ds(pl.multiple_of(half * half_d + chunk * rows, rows), rows)
        there = pl.ds(pl.multiple_of(chunk * rows, rows), rows)
        if part < 3:
            pairs = [(x_ref[:, here], y_ref[part]), (x_pair[:, there], y_pair[part])]
        else:
            pairs = [(y_ref[3], c_ref[:, here]), (y_pair[3], c_pair[:, there])]
        mine, other = [
            lax.dot_general(left, right, contract, preferred_element_type=jnp.float32)
            for left, right in pairs
        ]
        return mine + other

    def first_at(part):
        return first_q.at[part] if part < 3 else first_o

    def own_at(part):
        return own_q.at[part] if part < 3 else own_o

    def slot_at(step, part):
        return slots_q.at[step, part] if part < 3 else slots_o.at[step]

    def ring_copy(src, step, part):
        return remote(
            src, slot_at(step, part), rs_send.at[step, part], rs_recv.at[step, part], after
        )

    for part in order:
        if part == 3:
            needed = swaps[:2]
        elif part == 0:
            needed = swaps[2:4]
        else:
            needed = [swaps[3 + part]]
        for swap in needed:
            swap.wait_recv()
        first_at(part)[...] = product(me, part).astype(jnp.bfloat16)
        ring_copy(first_at(part), 0, part).start()

    def reduce_step(step, carry):
        chunk = lax.rem(me - step - 1 + count, count)
        for part in order:
            own_at(part)[...] = product(chunk, part)
        for part in order:
            slot = slot_at(step, part)
            ring_copy(first_at(part), step, part).wait_recv()
            slot[...] = (slot[...].astype(jnp.float32) + own_at(part)[...]).astype(jnp.bfloat16)

            @pl.when(step < count - 2)
            def _():
                ring_copy(slot_at(step, part), step + 1, part).start()

        return carry

    lax.fori_loop(0, count - 1, reduce_step, 0)

    def place(side, chunk, part):
        start = pl.multiple_of(side * half_d + chunk * rows, rows)
        if part < 3:
            return qkv_ref.at[part, pl.ds(start, rows)]
        return out_ref.at[:, pl.ds(start, rows)]

    done = lax.rem(me + 1, count)
    pending = []
    for part in order:
        final = slot_at(count - 2, part)
        target = place(half, done, part)
        spread = remote(final, target, ag_send.at[0, part], ag_recv.at[0, part], after)
        spread.start()
        share = remote(final, target, share_send.at[0, part], share_recv.at[0, part], partner)
        share.start()
        store = pltpu.make_async_copy(final, target, local_sem.at[part])
        store.start()
        pending.append((spread, share, store))

    def gain_copy(step):
        return remote(
            gain_acc.at[step],
            gain_slots.at[step],
            gain_send.at[step],
            gain_recv.at[step],
            friends[step],
        )

    gain_acc[0] = gain_ref[...]
    gain_copy(0).start()
    rounds = len(friends)

    def gain_round(step):
        gain_copy(step).wait_recv()
        gain_acc[step + 1] = gain_acc[step] + gain_slots[step]
        if step + 1 < rounds:
            gain_copy(step + 1).start()

    load = pltpu.make_async_copy(back_ref.at[outer], tile_in, local_sem.at[4])
    load.start()
    load.wait()
    tile_sum[...] = tile_in[...].astype(jnp.float32)
    for index in range(replicas - 1):
        back[index].wait_recv()
        load = pltpu.make_async_copy(shares_ref.at[index], tile_in, local_sem.at[5])
        load.start()
        load.wait()
        tile_sum[...] += tile_in[...].astype(jnp.float32)
    tile_low[...] = tile_sum[...].astype(jnp.bfloat16)
    keep = pltpu.make_async_copy(tile_low.at[0], got_ref.at[0], local_sem.at[6])
    keep.start()
    halos = []
    for index, (a, b) in enumerate(moves):
        block = 2 * a + b
        push = remote(
            tile_low.at[block],
            got_ref.at[block],
            back_send.at[index],
            back_recv.at[index],
            halo_to[index],
        )
        push.start()
        halos.append(push)

    def finish(block):
        if block == 0:
            keep.wait()
        else:
            halos[block - 1].wait_recv()
        back_values = got_ref[block].astype(jnp.float32)
        values = token_ref[block].astype(jnp.float32)
        standard, inverse_std = standardize(values)
        output_ref[block] = (values + back_values[:PART]).astype(jnp.bfloat16)
        scaled = back_values[PART:] * norm_ref[...]
        d_local = inverse_std * (
            scaled
            - jnp.mean(scaled, -1, keepdims=True)
            - standard * jnp.mean(scaled * standard, -1, keepdims=True)
        )
        d_tokens_ref[block] = (grad_ref[block].astype(jnp.float32) + d_local).astype(jnp.bfloat16)

    sends = []
    for step in range(count - 1):
        chunk = lax.rem(me - step + count, count)
        for part in order:
            here = place(half, chunk, part)
            remote(
                slot_at(count - 2, part), here, ag_send.at[step, part], ag_recv.at[step, part], after
            ).wait_recv()
            if step < count - 2:
                spread = remote(
                    here, here, ag_send.at[step + 1, part], ag_recv.at[step + 1, part], after
                )
                spread.start()
                sends.append(spread)
            share = remote(
                here, here, share_send.at[step + 1, part], share_recv.at[step + 1, part], partner
            )
            share.start()
            sends.append(share)
        if step < rounds:
            gain_round(step)
        if 3 <= step < 7:
            finish(step - 3)
    for step in range(count - 1, rounds):
        gain_round(step)
    gain_out[...] = gain_acc[rounds]

    partner_me = jnp.where(half == 0, count - 1 - spot, spot)
    for step in range(count):
        chunk = lax.rem(partner_me + 1 - step + count, count)
        for part in range(4):
            remote(
                slot_at(count - 2, part),
                place(1 - half, chunk, part),
                share_send.at[step, part],
                share_recv.at[step, part],
                partner,
            ).wait_recv()
    for push in halos:
        push.wait_send()
    for push in back:
        push.wait_send()
    for swap in swaps:
        swap.wait_send()
    for part in range(4):
        ring_copy(first_at(part), 0, part).wait_send()

    def drain(step, carry):
        for part in range(4):
            ring_copy(slot_at(step, part), step + 1, part).wait_send()
        return carry

    lax.fori_loop(0, count - 2, drain, 0)
    for spread, share, store in pending:
        spread.wait_send()
        share.wait_send()
        store.wait()
    for copy in sends:
        copy.wait_send()
    for step in range(rounds):
        gain_copy(step).wait_send()


def grads_exchange(sizes, x, c, y, gain, token_blocks, grad_blocks, norm_gain, back):
    replicas, n_lat, n_lon = sizes
    count = n_lat // 2 * n_lon
    rows = D // 2 // count
    tokens, heads_dev = y.shape[1:]
    friends = sum(size.bit_length() - 1 for size in sizes)
    dma = pltpu.SemaphoreType.DMA
    vmem = pl.BlockSpec(memory_space=pltpu.VMEM)
    hbm = pl.BlockSpec(memory_space=pl.ANY)
    low, wide = jnp.bfloat16, jnp.float32
    return pl.pallas_call(
        functools.partial(grads_kernel, sizes),
        out_shape=(
            jax.ShapeDtypeStruct((3, D, heads_dev), low),
            jax.ShapeDtypeStruct((heads_dev, D), low),
            jax.ShapeDtypeStruct((replicas - 1, 4, PAIR, D), low),
            jax.ShapeDtypeStruct((D // 128, 128), wide),
            jax.ShapeDtypeStruct((4, PART, D), low),
            jax.ShapeDtypeStruct((4, PART, D), low),
        ),
        in_specs=[vmem] * 7 + [hbm],
        out_specs=(hbm, hbm, hbm, vmem, vmem, vmem),
        scratch_shapes=[
            pltpu.VMEM((tokens, D // 2), low),
            pltpu.VMEM((tokens, D // 2), low),
            pltpu.VMEM((4, tokens, heads_dev), low),
            pltpu.VMEM((3, rows, heads_dev), low),
            pltpu.VMEM((heads_dev, rows), low),
            pltpu.VMEM((count - 1, 3, rows, heads_dev), low),
            pltpu.VMEM((count - 1, heads_dev, rows), low),
            pltpu.VMEM((3, rows, heads_dev), wide),
            pltpu.VMEM((heads_dev, rows), wide),
            pltpu.VMEM((friends + 1, D // 128, 128), wide),
            pltpu.VMEM((friends, D // 128, 128), wide),
            pltpu.VMEM((4, PAIR, D), low),
            pltpu.VMEM((4, PAIR, D), wide),
            pltpu.VMEM((4, PAIR, D), low),
            pltpu.VMEM((4, PAIR, D), low),
            dma((6,)),
            dma((6,)),
            dma((count - 1, 4)),
            dma((count - 1, 4)),
            dma((count - 1, 4)),
            dma((count - 1, 4)),
            dma((count, 4)),
            dma((count, 4)),
            dma((replicas - 1,)),
            dma((replicas - 1,)),
            dma((3,)),
            dma((3,)),
            dma((friends,)),
            dma((friends,)),
            dma((7,)),
        ],
        compiler_params=pltpu.CompilerParams(
            collective_id=2, has_side_effects=True, vmem_limit_bytes=60 * 1024 * 1024
        ),
    )(x, c, y, gain, token_blocks, grad_blocks, norm_gain, back)


def attention_kernel(
    group,
    blocked_ref,
    arrived_ref,
    w_ref,
    out_w_ref,
    gain_ref,
    y_ref,
    x_ref,
    c_ref,
    back_ref,
    gain_out,
    q_low,
    k_low,
    v_low,
    d_low,
    branch_acc,
    rolled_acc,
):
    step = pl.program_id(1)

    @pl.when(step == 0)
    def _():
        for window in range(group):
            parts = [arrived_ref[window, block].astype(jnp.float32) for block in range(4)]
            at = slice(window * TILE, (window + 1) * TILE)
            x_ref[at] = jnp.concatenate([part[:PART] for part in parts], 0).astype(jnp.bfloat16)
            c_ref[at] = jnp.concatenate([part[PART:] for part in parts], 0).astype(jnp.bfloat16)

    scale = HEAD ** (-0.5)
    width = w_ref.shape[2]
    x, c = x_ref[...], c_ref[...]
    for index, target in enumerate((q_low, k_low, v_low)):
        target[...] = jnp.dot(x, w_ref[index], preferred_element_type=jnp.float32).astype(
            jnp.bfloat16
        )
    d_low[...] = contract_cols(c, out_w_ref[...]).astype(jnp.bfloat16)
    lane = lax.broadcasted_iota(jnp.int32, (TILE, 128), 1)
    lower = lane < HEAD
    contract = (((0,), (0,)), ((), ()))
    for window in range(group):
        blocked = blocked_ref[window] < 0
        at = slice(window * TILE, (window + 1) * TILE)
        for pair in range(width // 128):
            cols = slice(pair * 128, (pair + 1) * 128)
            q, k, v, d = q_low[at, cols], k_low[at, cols], v_low[at, cols], d_low[at, cols]
            results = []
            for head in range(2):
                mine = lower if head == 0 else jnp.logical_not(lower)
                q_head = jnp.where(mine, q, jnp.zeros_like(q))
                d_head = jnp.where(mine, d, jnp.zeros_like(d))
                scores = jnp.where(blocked, -1e30, contract_cols(q_head, k) * scale)
                exponent = jnp.exp(scores - jnp.max(scores, -1, keepdims=True))
                weights = exponent / jnp.sum(exponent, -1, keepdims=True)
                weights_low = weights.astype(jnp.bfloat16)
                d_weights = contract_cols(d_head, v)
                row_dots = jnp.sum(weights * d_weights, -1, keepdims=True)
                d_scores = (weights * (d_weights - row_dots) * scale).astype(jnp.bfloat16)
                results.append(
                    (
                        jnp.dot(d_scores, k, preferred_element_type=jnp.float32),
                        lax.dot_general(
                            d_scores, q, contract, preferred_element_type=jnp.float32
                        ),
                        lax.dot_general(
                            weights_low, d, contract, preferred_element_type=jnp.float32
                        ),
                        jnp.dot(weights_low, v, preferred_element_type=jnp.float32),
                    )
                )
            for index in range(4):
                y_ref[index, at, cols] = jnp.where(
                    lower, results[0][index], results[1][index]
                ).astype(jnp.bfloat16)

    branch = jnp.dot(y_ref[3], out_w_ref[...], preferred_element_type=jnp.float32)
    rolled = contract_cols(y_ref[0], w_ref[0])
    rolled += contract_cols(y_ref[1], w_ref[1])
    rolled += contract_cols(y_ref[2], w_ref[2])

    @pl.when(step == 0)
    def _():
        branch_acc[...] = branch
        rolled_acc[...] = rolled

    @pl.when(step > 0)
    def _():
        branch_acc[...] += branch
        rolled_acc[...] += rolled

    @pl.when(step == pl.num_programs(1) - 1)
    def _():
        for window in range(group):
            for block in range(4):
                start = window * TILE + block * PART
                at = slice(start, start + PART)
                both = jnp.concatenate([branch_acc[at], rolled_acc[at]], axis=0)
                back_ref[window, block] = both.astype(jnp.bfloat16)
        low = rolled_acc[...].astype(jnp.bfloat16)
        product = low.astype(jnp.float32) * x_ref[...].astype(jnp.float32)
        gain_out[0] = jnp.sum(product, 0, keepdims=True) / gain_ref[...]


def attention(arrived, w_three, w_out, gain, blocked):
    replicas = arrived.shape[0]
    total = replicas * TILE
    heads_dev = w_three.shape[2]
    width = min(256, heads_dev)
    group = 2
    tile = group * TILE
    low, wide = jnp.bfloat16, jnp.float32
    return pl.pallas_call(
        functools.partial(attention_kernel, group),
        grid=(total // tile, heads_dev // width),
        in_specs=[
            pl.BlockSpec((group, TILE, TILE), lambda g, j: (g, 0, 0)),
            pl.BlockSpec((group, 4, PAIR, D), lambda g, j: (g, 0, 0, 0)),
            pl.BlockSpec((3, D, width), lambda g, j: (0, 0, j)),
            pl.BlockSpec((width, D), lambda g, j: (j, 0)),
            pl.BlockSpec((1, D), lambda g, j: (0, 0)),
        ],
        out_specs=(
            pl.BlockSpec((4, tile, width), lambda g, j: (0, g, j)),
            pl.BlockSpec((tile, D), lambda g, j: (g, 0)),
            pl.BlockSpec((tile, D), lambda g, j: (g, 0)),
            pl.BlockSpec((group, 4, PAIR, D), lambda g, j: (g, 0, 0, 0)),
            pl.BlockSpec((1, 1, D), lambda g, j: (g, 0, 0)),
        ),
        out_shape=(
            jax.ShapeDtypeStruct((4, total, heads_dev), low),
            jax.ShapeDtypeStruct((total, D), low),
            jax.ShapeDtypeStruct((total, D), low),
            jax.ShapeDtypeStruct((replicas, 4, PAIR, D), low),
            jax.ShapeDtypeStruct((total // tile, 1, D), wide),
        ),
        scratch_shapes=[pltpu.VMEM((tile, width), low)] * 4 + [pltpu.VMEM((tile, D), wide)] * 2,
        compiler_params=pltpu.CompilerParams(
            dimension_semantics=("arbitrary", "arbitrary"), vmem_limit_bytes=48 * 1024 * 1024
        ),
    )(blocked, arrived, w_three, w_out, gain)


def block_kernel(
    sizes,
    blocked_ref,
    token_ref,
    grad_ref,
    gain_ref,
    w_ref,
    out_w_ref,
    y_ref,
    x_ref,
    c_ref,
    back_ref,
    gain_out,
    src,
    arrived,
    q_low,
    k_low,
    v_low,
    d_low,
    att_low,
    weights_ref,
    branch_acc,
    rolled_acc,
    send_sem,
    recv_sem,
):
    group = sizes[0]
    step = pl.program_id(0)
    steps = pl.num_programs(0) // 2
    column = lax.rem(step, steps)
    scale = HEAD ** (-0.5)
    width = w_ref.shape[2]
    routes = gather_routes(sizes)
    routes = [r for r in routes if (r[0], r[1]) != (0, 0)]
    routes = [r for r in routes if r[0] > 0] + [r for r in routes if r[0] == 0]
    outer, _, _ = position()
    ranges = (pl.ds(0, 48), pl.ds(48, 32))

    def front_copy(index, part, tile):
        _, block, target, _, _, _ = routes[index]
        return pltpu.make_async_remote_copy(
            src.at[block, ranges[part]],
            arrived.at[tile, block, ranges[part]],
            send_sem.at[part, index],
            recv_sem.at[part, index],
            device_id=target,
            device_id_type=MESH,
        )

    @pl.when(step == 0)
    def _():
        for block in range(4):
            standard, _ = standardize(token_ref[block].astype(jnp.float32))
            both = [standard * gain_ref[...], grad_ref[block].astype(jnp.float32)]
            src[block] = jnp.concatenate(both, axis=0).astype(jnp.bfloat16)
        enter([r[2] for r in routes], [r[4] for r in routes])
        for part in range(2):
            for index, route in enumerate(routes):
                front_copy(index, part, route[3]).start()
        arrived[outer, 0] = src[0]
        for index, route in enumerate(routes):
            front_copy(index, 0, route[5]).wait_recv()
        for window in range(group):
            parts = [arrived[window, b, :48].astype(jnp.float32)[:PART] for b in range(4)]
            at = slice(window * TILE, (window + 1) * TILE)
            x_ref[at] = jnp.concatenate(parts, 0).astype(jnp.bfloat16)

    @pl.when(step == steps)
    def _():
        for index, route in enumerate(routes):
            front_copy(index, 1, route[5]).wait_recv()
        for part in range(2):
            for index, route in enumerate(routes):
                front_copy(index, part, route[3]).wait_send()
        for window in range(group):
            parts = [arrived[window, b].astype(jnp.float32)[PART:] for b in range(4)]
            at = slice(window * TILE, (window + 1) * TILE)
            c_ref[at] = jnp.concatenate(parts, 0).astype(jnp.bfloat16)

    lower = lax.broadcasted_iota(jnp.int32, (TILE, 128), 1) < HEAD
    contract = (((0,), (0,)), ((), ()))
    units = [(window, pair) for window in range(group) for pair in range(width // 128)]

    def region(window, pair):
        return (
            slice(window * TILE, (window + 1) * TILE),
            slice(pair * 128, (pair + 1) * 128),
        )

    @pl.when(step < steps)
    def _():
        x = x_ref[...]
        for index, target in enumerate((q_low, k_low, v_low)):
            target[column] = jnp.dot(
                x, w_ref[index], preferred_element_type=jnp.float32
            ).astype(jnp.bfloat16)
        for unit, (window, pair) in enumerate(units):
            blocked = blocked_ref[window] < 0
            at, cols = region(window, pair)
            q, k, v = q_low[column, at, cols], k_low[column, at, cols], v_low[column, at, cols]
            results = []
            for head in range(2):
                mine = lower if head == 0 else jnp.logical_not(lower)
                q_head = jnp.where(mine, q, jnp.zeros_like(q))
                scores = jnp.where(blocked, -1e30, contract_cols(q_head, k) * scale)
                exponent = jnp.exp(scores - jnp.max(scores, -1, keepdims=True))
                weights = exponent / jnp.sum(exponent, -1, keepdims=True)
                weights_ref[column, 2 * unit + head] = weights
                results.append(
                    jnp.dot(weights.astype(jnp.bfloat16), v, preferred_element_type=jnp.float32)
                )
            att_low[column, at, cols] = jnp.where(lower, results[0], results[1]).astype(
                jnp.bfloat16
            )

    @pl.when(step >= steps)
    def _():
        d_low[...] = contract_cols(c_ref[...], out_w_ref[...]).astype(jnp.bfloat16)
        for unit, (window, pair) in enumerate(units):
            at, cols = region(window, pair)
            q, k, v = q_low[column, at, cols], k_low[column, at, cols], v_low[column, at, cols]
            d = d_low[at, cols]
            results = []
            for head in range(2):
                mine = lower if head == 0 else jnp.logical_not(lower)
                d_head = jnp.where(mine, d, jnp.zeros_like(d))
                weights = weights_ref[column, 2 * unit + head]
                weights_low = weights.astype(jnp.bfloat16)
                d_weights = contract_cols(d_head, v)
                row_dots = jnp.sum(weights * d_weights, -1, keepdims=True)
                d_scores = (weights * (d_weights - row_dots) * scale).astype(jnp.bfloat16)
                results.append(
                    (
                        jnp.dot(d_scores, k, preferred_element_type=jnp.float32),
                        lax.dot_general(
                            d_scores, q, contract, preferred_element_type=jnp.float32
                        ),
                        lax.dot_general(
                            weights_low, d, contract, preferred_element_type=jnp.float32
                        ),
                    )
                )
            for index in range(3):
                y_ref[index, at, cols] = jnp.where(
                    lower, results[0][index], results[1][index]
                ).astype(jnp.bfloat16)
        y_ref[3] = att_low[column]
        branch = jnp.dot(y_ref[3], out_w_ref[...], preferred_element_type=jnp.float32)
        rolled = contract_cols(y_ref[0], w_ref[0])
        rolled += contract_cols(y_ref[1], w_ref[1])
        rolled += contract_cols(y_ref[2], w_ref[2])

        @pl.when(step == steps)
        def _():
            branch_acc[...] = branch
            rolled_acc[...] = rolled

        @pl.when(step > steps)
        def _():
            branch_acc[...] += branch
            rolled_acc[...] += rolled

    @pl.when(step == 2 * steps - 1)
    def _():
        for window in range(group):
            for block in range(4):
                start = window * TILE + block * PART
                at = slice(start, start + PART)
                both = jnp.concatenate([branch_acc[at], rolled_acc[at]], axis=0)
                back_ref[window, block] = both.astype(jnp.bfloat16)
        low = rolled_acc[...].astype(jnp.bfloat16)
        product = low.astype(jnp.float32) * x_ref[...].astype(jnp.float32)
        gain_out[0] = jnp.sum(product, 0, keepdims=True) / gain_ref[...]


def front_and_attention(sizes, token_blocks, grad_blocks, w_three, w_out, gain, blocked):
    replicas = sizes[0]
    total = replicas * TILE
    heads_dev = w_three.shape[2]
    width = min(256, heads_dev)
    steps = heads_dev // width
    count = 4 * replicas - 1
    low, wide = jnp.bfloat16, jnp.float32

    def later(i):
        return jnp.maximum(i - steps, 0)

    def whole(*shape):
        return pl.BlockSpec(shape, lambda i: (0,) * len(shape))

    return pl.pallas_call(
        functools.partial(block_kernel, sizes),
        grid=(2 * steps,),
        in_specs=[
            whole(replicas, TILE, TILE),
            whole(4, PART, D),
            whole(4, PART, D),
            whole(1, D),
            pl.BlockSpec((3, D, width), lambda i: (0, 0, lax.rem(i, steps))),
            pl.BlockSpec((width, D), lambda i: (later(i), 0)),
        ],
        out_specs=(
            pl.BlockSpec((4, total, width), lambda i: (0, 0, later(i))),
            whole(total, D),
            whole(total, D),
            whole(replicas, 4, PAIR, D),
            whole(1, 1, D),
        ),
        out_shape=(
            jax.ShapeDtypeStruct((4, total, heads_dev), low),
            jax.ShapeDtypeStruct((total, D), low),
            jax.ShapeDtypeStruct((total, D), low),
            jax.ShapeDtypeStruct((replicas, 4, PAIR, D), low),
            jax.ShapeDtypeStruct((1, 1, D), wide),
        ),
        scratch_shapes=[
            pltpu.VMEM((4, PAIR, D), low),
            pltpu.VMEM((replicas, 4, PAIR, D), low),
            pltpu.VMEM((steps, total, width), low),
            pltpu.VMEM((steps, total, width), low),
            pltpu.VMEM((steps, total, width), low),
            pltpu.VMEM((total, width), low),
            pltpu.VMEM((steps, total, width), low),
            pltpu.VMEM((steps, replicas * width // HEAD, TILE, TILE), wide),
            pltpu.VMEM((total, D), wide),
            pltpu.VMEM((total, D), wide),
            pltpu.SemaphoreType.DMA((2, count)),
            pltpu.SemaphoreType.DMA((2, count)),
        ],
        compiler_params=pltpu.CompilerParams(
            collective_id=3,
            has_side_effects=True,
            dimension_semantics=("arbitrary",),
            vmem_limit_bytes=56 * 1024 * 1024,
        ),
    )(blocked, token_blocks, grad_blocks, gain, w_three, w_out)


def contract_cols(left, right):
    return lax.dot_general(
        left, right, (((1,), (1,)), ((), ())), preferred_element_type=jnp.float32
    )


def to_blocks(tensor):
    shaped = tensor.reshape(2, CLAT, 2, WLON // 2, LEV, D)
    blocks = [shaped[1 - a, :, 1 - b].reshape(QUARTER, D) for a in range(2) for b in range(2)]
    return jnp.pad(jnp.stack(blocks), ((0, 0), (0, PART - QUARTER), (0, 0)))


def from_blocks(blocks):
    shaped = blocks[:, :QUARTER].reshape(2, 2, CLAT, WLON // 2, LEV, D)
    rows = [jnp.concatenate([shaped[a, 1], shaped[a, 0]], axis=1) for a in (1, 0)]
    return jnp.concatenate(rows, axis=0)


def shards(tokens, norm_gain, w_qkv, w_out, grad_out):
    sizes = tuple(lax.axis_size(name) for name in ("outer", "lat", "lon"))
    replicas, lat_count, lon_count = sizes
    assert tokens.shape[:3] == (2 * CLAT, LEV, WLON)
    lat_index = lax.axis_index("lat")
    w_three = w_qkv.transpose(1, 0, 2)
    gain = norm_gain.reshape(1, D)
    token_blocks = to_blocks(tokens.transpose(0, 2, 1, 3))
    grad_blocks = to_blocks(grad_out.transpose(0, 2, 1, 3))
    cut_window = jnp.logical_and(lat_index == lat_count - 1, jnp.arange(replicas) == replicas - 1)
    spot = jnp.arange(TILE)
    half_index = spot // (2 * PART)
    other_half = half_index[:, None] != half_index[None, :]
    blocked = jnp.logical_and(cut_window[:, None, None], other_half[None])
    blocked = jnp.logical_or(blocked, (spot % PART >= QUARTER)[None, None])
    blocked = jnp.where(blocked, -1.0, 0.0).astype(jnp.float32)
    if replicas == 2:
        y, x, c, back, gain_local = front_and_attention(
            sizes, token_blocks, grad_blocks, w_three, w_out, gain, blocked
        )
    else:
        arrived = front_exchange(sizes, token_blocks, grad_blocks, gain)
        y, x, c, back, gain_local = attention(arrived, w_three, w_out, gain, blocked)
    gain_local = jnp.sum(gain_local, (0, 1)).reshape(D // 128, 128)
    grad_qkv, grad_out_w, _, grad_gain, output, grad_tokens = grads_exchange(
        sizes, x, c, y, gain_local, token_blocks, grad_blocks, gain, back
    )
    grad_wqkv = grad_qkv.astype(jnp.float32).transpose(1, 0, 2)
    grad_wout = grad_out_w.astype(jnp.float32)
    return (
        from_blocks(output).transpose(0, 2, 1, 3),
        from_blocks(grad_tokens).transpose(0, 2, 1, 3),
        grad_wqkv,
        grad_wout,
        grad_gain.reshape(D),
    )


def solution(mesh):
    in_specs = (
        P(("outer", "lat"), None, "lon", None),
        P(),
        P(None, None, "outer"),
        P("outer", None),
        P(("outer", "lat"), None, "lon", None),
    )
    out_specs = (
        P(("outer", "lat"), None, "lon", None),
        P(("outer", "lat"), None, "lon", None),
        P(None, None, "outer"),
        P("outer", None),
        P(),
    )
    return jax.shard_map(shards, mesh=mesh, in_specs=in_specs, out_specs=out_specs, check_vma=False)
```

```python
import functools

import jax
import jax.numpy as jnp
from jax import lax
from jax.experimental import pallas as pl
from jax.experimental.pallas import tpu as pltpu
from jax.sharding import PartitionSpec as P

D = 2048
HEAD = 64
LEV = 2
CLAT = 3
WLON = 12
QUARTER = CLAT * LEV * WLON // 2
PART = 40
PAIR = 2 * PART
TILE = 4 * PART
MESH = pl.DeviceIdType.MESH
epsilon = 1e-05


def position():
    return lax.axis_index("outer"), lax.axis_index("lat"), lax.axis_index("lon")


def enter(receivers, senders):
    barrier = pltpu.get_barrier_semaphore()
    for device in senders:
        pl.semaphore_signal(barrier, inc=1, device_id=device, device_id_type=MESH)
    pl.semaphore_wait(barrier, len(receivers))


def shifted(sizes, band, lat, lon, rows, columns):
    replicas, n_lat, n_lon = sizes
    flat = lax.rem(band * n_lat + lat + rows + replicas * n_lat, replicas * n_lat)
    return flat // n_lat, lax.rem(flat, n_lat), lax.rem(lon + columns + n_lon, n_lon)


def gather_routes(sizes):
    outer, lat, lon = position()
    routes = []
    for step in range(sizes[0]):
        for a in range(2):
            for b in range(2):
                band, lat_to, lon_to = shifted(sizes, outer, lat, lon, -a, -b)
                group = lax.rem(band + step, sizes[0])
                band_from, lat_from, lon_from = shifted(sizes, outer, lat, lon, a, b)
                tile_from = lax.rem(outer - step + sizes[0], sizes[0])
                source_band, source_lat, source_lon = shifted(sizes, tile_from, lat, lon, a, b)
                routes.append(
                    (
                        step,
                        2 * a + b,
                        (group, lat_to, lon_to),
                        band,
                        (source_band, source_lat, source_lon),
                        tile_from,
                    )
                )
    return routes


def standardize(values):
    centered = values - jnp.mean(values, -1, keepdims=True)
    inverse_std = lax.rsqrt(jnp.mean(centered * centered, -1, keepdims=True) + epsilon)
    return centered * inverse_std, inverse_std


def front_kernel(sizes, token_ref, grad_ref, gain_ref, got, src, send_sem, recv_sem, local_sem):
    for block in range(4):
        standard, _ = standardize(token_ref[block].astype(jnp.float32))
        both = [standard * gain_ref[...], grad_ref[block].astype(jnp.float32)]
        src[block] = jnp.concatenate(both, axis=0).astype(jnp.bfloat16)
    routes = gather_routes(sizes)
    remote = [r for r in routes if (r[0], r[1]) != (0, 0)]
    remote = [r for r in remote if r[0] > 0] + [r for r in remote if r[0] == 0]
    enter([r[2] for r in remote], [r[4] for r in remote])
    outer, _, _ = position()
    copies = []
    for index, (step, block, target, tile, _, tile_from) in enumerate(remote):
        push = pltpu.make_async_remote_copy(
            src.at[block],
            got.at[tile, block],
            send_sem.at[index],
            recv_sem.at[index],
            device_id=target,
            device_id_type=MESH,
        )
        push.start()
        arrive = pltpu.make_async_remote_copy(
            src.at[block],
            got.at[tile_from, block],
            send_sem.at[index],
            recv_sem.at[index],
            device_id=target,
            device_id_type=MESH,
        )
        copies.append((push, arrive))
    own = pltpu.make_async_copy(src.at[0], got.at[outer, 0], local_sem)
    own.start()
    for push, arrive in copies:
        arrive.wait_recv()
    for push, arrive in copies:
        push.wait_send()
    own.wait()


def front_exchange(sizes, token_blocks, grad_blocks, gain):
    replicas = sizes[0]
    count = 4 * replicas - 1
    return pl.pallas_call(
        functools.partial(front_kernel, sizes),
        out_shape=jax.ShapeDtypeStruct((replicas, 4, PAIR, D), jnp.bfloat16),
        in_specs=[pl.BlockSpec(memory_space=pltpu.VMEM)] * 3,
        out_specs=pl.BlockSpec(memory_space=pl.ANY),
        scratch_shapes=[
            pltpu.VMEM((4, PAIR, D), jnp.bfloat16),
            pltpu.SemaphoreType.DMA((count,)),
            pltpu.SemaphoreType.DMA((count,)),
            pltpu.SemaphoreType.DMA(()),
        ],
        compiler_params=pltpu.CompilerParams(
            collective_id=1, has_side_effects=True, vmem_limit_bytes=32 * 1024 * 1024
        ),
    )(token_blocks, grad_blocks, gain)


def xor_partners(sizes):
    outer, lat, lon = position()
    result = []
    for axis, size in enumerate(sizes):
        bit = 1
        while bit < size:
            at = [outer, lat, lon]
            lower = lax.rem(at[axis] // bit, 2)
            at[axis] = at[axis] + bit * (1 - 2 * lower)
            result.append(tuple(at))
            bit *= 2
    return result


def grads_kernel(
    sizes,
    x_ref,
    c_ref,
    y_ref,
    gain_ref,
    token_ref,
    grad_ref,
    norm_ref,
    back_ref,
    qkv_ref,
    out_ref,
    shares_ref,
    gain_out,
    output_ref,
    d_tokens_ref,
    x_pair,
    c_pair,
    y_pair,
    first_q,
    first_o,
    slots_q,
    slots_o,
    own_q,
    own_o,
    gain_acc,
    gain_slots,
    tile_in,
    tile_sum,
    tile_low,
    got_ref,
    pair_send,
    pair_recv,
    rs_send,
    rs_recv,
    ag_send,
    ag_recv,
    share_send,
    share_recv,
    outer_send,
    outer_recv,
    back_send,
    back_recv,
    gain_send,
    gain_recv,
    local_sem,
):
    replicas, n_lat, n_lon = sizes
    outer, lat, lon = position()
    count = n_lat // 2 * n_lon
    rows = D // 2 // count
    half = lax.rem(lat, 2)
    upper = lat // 2
    partner = (outer, lat + 1 - 2 * half, lon)

    def on_ring(place):
        place = lax.rem(place + count, count)
        turned = jnp.where(half == 0, place, count - 1 - place)
        row = turned // n_lon
        column = lax.rem(turned, n_lon)
        return (outer, 2 * row + half, jnp.where(lax.rem(row, 2) == 0, column, n_lon - 1 - column))

    along = jnp.where(lax.rem(upper, 2) == 0, lon, n_lon - 1 - lon)
    spot = upper * n_lon + along
    me = jnp.where(half == 0, spot, count - 1 - spot)
    after, before = on_ring(me + 1), on_ring(me - 1)

    groups_to = [(lax.rem(outer + step, replicas), lat, lon) for step in range(1, replicas)]
    groups_from = [
        (lax.rem(outer - step + replicas, replicas), lat, lon) for step in range(1, replicas)
    ]
    moves = [(0, 1), (1, 0), (1, 1)]
    halo_to = [shifted(sizes, outer, lat, lon, a, b) for a, b in moves]
    halo_from = [shifted(sizes, outer, lat, lon, -a, -b) for a, b in moves]
    friends = xor_partners(sizes)
    enter(
        [after, partner] + groups_to + halo_to + friends,
        [before, partner] + groups_from + halo_from + friends,
    )

    def remote(src, dst, send, recv, device):
        return pltpu.make_async_remote_copy(
            src, dst, send, recv, device_id=device, device_id_type=MESH
        )

    order = (3, 0, 1, 2)
    half_d = D // 2
    theirs = pl.ds(pl.multiple_of((1 - half) * half_d, half_d), half_d)
    swaps = [
        remote(c_ref.at[:, theirs], c_pair, pair_send.at[0], pair_recv.at[0], partner),
        remote(x_ref.at[:, theirs], x_pair, pair_send.at[1], pair_recv.at[1], partner),
    ]
    for index, part in enumerate(order):
        copy = remote(
            y_ref.at[part], y_pair.at[part], pair_send.at[2 + index], pair_recv.at[2 + index], partner
        )
        swaps.append(copy)
    swaps = [swaps[0], swaps[2], swaps[1]] + swaps[3:]
    for swap in swaps:
        swap.start()
    back = []
    for index, target in enumerate(groups_to):
        push = remote(
            back_ref.at[target[0]],
            shares_ref.at[index],
            outer_send.at[index],
            outer_recv.at[index],
            target,
        )
        push.start()
        back.append(push)
    contract = (((0,), (0,)), ((), ()))

    def product(chunk, part):
        here = pl.ds(pl.multiple_of(half * half_d + chunk * rows, rows), rows)
        there = pl.ds(pl.multiple_of(chunk * rows, rows), rows)
        if part < 3:
            pairs = [(x_ref[:, here], y_ref[part]), (x_pair[:, there], y_pair[part])]
        else:
            pairs = [(y_ref[3], c_ref[:, here]), (y_pair[3], c_pair[:, there])]
        mine, other = [
            lax.dot_general(left, right, contract, preferred_element_type=jnp.float32)
            for left, right in pairs
        ]
        return mine + other

    def first_at(part):
        return first_q.at[part] if part < 3 else first_o

    def own_at(part):
        return own_q.at[part] if part < 3 else own_o

    def slot_at(step, part):
        return slots_q.at[step, part] if part < 3 else slots_o.at[step]

    def ring_copy(src, step, part):
        return remote(
            src, slot_at(step, part), rs_send.at[step, part], rs_recv.at[step, part], after
        )

    for part in order:
        if part == 3:
            needed = swaps[:2]
        elif part == 0:
            needed = swaps[2:4]
        else:
            needed = [swaps[3 + part]]
        for swap in needed:
            swap.wait_recv()
        first_at(part)[...] = product(me, part).astype(jnp.bfloat16)
        ring_copy(first_at(part), 0, part).start()

    def reduce_step(step, carry):
        chunk = lax.rem(me - step - 1 + count, count)
        for part in order:
            own_at(part)[...] = product(chunk, part)
        for part in order:
            slot = slot_at(step, part)
            ring_copy(first_at(part), step, part).wait_recv()
            slot[...] = (slot[...].astype(jnp.float32) + own_at(part)[...]).astype(jnp.bfloat16)

            @pl.when(step < count - 2)
            def _():
                ring_copy(slot_at(step, part), step + 1, part).start()

        return carry

    lax.fori_loop(0, count - 1, reduce_step, 0)

    def place(side, chunk, part):
        start = pl.multiple_of(side * half_d + chunk * rows, rows)
        if part < 3:
            return qkv_ref.at[part, pl.ds(start, rows)]
        return out_ref.at[:, pl.ds(start, rows)]

    done = lax.rem(me + 1, count)
    pending = []
    for part in order:
        final = slot_at(count - 2, part)
        target = place(half, done, part)
        spread = remote(final, target, ag_send.at[0, part], ag_recv.at[0, part], after)
        spread.start()
        share = remote(final, target, share_send.at[0, part], share_recv.at[0, part], partner)
        share.start()
        store = pltpu.make_async_copy(final, target, local_sem.at[part])
        store.start()
        pending.append((spread, share, store))

    def gain_copy(step):
        return remote(
            gain_acc.at[step],
            gain_slots.at[step],
            gain_send.at[step],
            gain_recv.at[step],
            friends[step],
        )

    gain_acc[0] = gain_ref[...]
    gain_copy(0).start()
    rounds = len(friends)

    def gain_round(step):
        gain_copy(step).wait_recv()
        gain_acc[step + 1] = gain_acc[step] + gain_slots[step]
        if step + 1 < rounds:
            gain_copy(step + 1).start()

    load = pltpu.make_async_copy(back_ref.at[outer], tile_in, local_sem.at[4])
    load.start()
    load.wait()
    tile_sum[...] = tile_in[...].astype(jnp.float32)
    for index in range(replicas - 1):
        back[index].wait_recv()
        load = pltpu.make_async_copy(shares_ref.at[index], tile_in, local_sem.at[5])
        load.start()
        load.wait()
        tile_sum[...] += tile_in[...].astype(jnp.float32)
    tile_low[...] = tile_sum[...].astype(jnp.bfloat16)
    keep = pltpu.make_async_copy(tile_low.at[0], got_ref.at[0], local_sem.at[6])
    keep.start()
    halos = []
    for index, (a, b) in enumerate(moves):
        block = 2 * a + b
        push = remote(
            tile_low.at[block],
            got_ref.at[block],
            back_send.at[index],
            back_recv.at[index],
            halo_to[index],
        )
        push.start()
        halos.append(push)

    def finish(block):
        if block == 0:
            keep.wait()
        else:
            halos[block - 1].wait_recv()
        back_values = got_ref[block].astype(jnp.float32)
        values = token_ref[block].astype(jnp.float32)
        standard, inverse_std = standardize(values)
        output_ref[block] = (values + back_values[:PART]).astype(jnp.bfloat16)
        scaled = back_values[PART:] * norm_ref[...]
        d_local = inverse_std * (
            scaled
            - jnp.mean(scaled, -1, keepdims=True)
            - standard * jnp.mean(scaled * standard, -1, keepdims=True)
        )
        d_tokens_ref[block] = (grad_ref[block].astype(jnp.float32) + d_local).astype(jnp.bfloat16)

    sends = []
    for step in range(count - 1):
        chunk = lax.rem(me - step + count, count)
        for part in order:
            here = place(half, chunk, part)
            remote(
                slot_at(count - 2, part), here, ag_send.at[step, part], ag_recv.at[step, part], after
            ).wait_recv()
            if step < count - 2:
                spread = remote(
                    here, here, ag_send.at[step + 1, part], ag_recv.at[step + 1, part], after
                )
                spread.start()
                sends.append(spread)
            share = remote(
                here, here, share_send.at[step + 1, part], share_recv.at[step + 1, part], partner
            )
            share.start()
            sends.append(share)
        if step < rounds:
            gain_round(step)
        if 3 <= step < 7:
            finish(step - 3)
    for step in range(count - 1, rounds):
        gain_round(step)
    gain_out[...] = gain_acc[rounds]

    partner_me = jnp.where(half == 0, count - 1 - spot, spot)
    for step in range(count):
        chunk = lax.rem(partner_me + 1 - step + count, count)
        for part in range(4):
            remote(
                slot_at(count - 2, part),
                place(1 - half, chunk, part),
                share_send.at[step, part],
                share_recv.at[step, part],
                partner,
            ).wait_recv()
    for push in halos:
        push.wait_send()
    for push in back:
        push.wait_send()
    for swap in swaps:
        swap.wait_send()
    for part in range(4):
        ring_copy(first_at(part), 0, part).wait_send()

    def drain(step, carry):
        for part in range(4):
            ring_copy(slot_at(step, part), step + 1, part).wait_send()
        return carry

    lax.fori_loop(0, count - 2, drain, 0)
    for spread, share, store in pending:
        spread.wait_send()
        share.wait_send()
        store.wait()
    for copy in sends:
        copy.wait_send()
    for step in range(rounds):
        gain_copy(step).wait_send()


def grads_exchange(sizes, x, c, y, gain, token_blocks, grad_blocks, norm_gain, back):
    replicas, n_lat, n_lon = sizes
    count = n_lat // 2 * n_lon
    rows = D // 2 // count
    tokens, heads_dev = y.shape[1:]
    friends = sum(size.bit_length() - 1 for size in sizes)
    dma = pltpu.SemaphoreType.DMA
    vmem = pl.BlockSpec(memory_space=pltpu.VMEM)
    hbm = pl.BlockSpec(memory_space=pl.ANY)
    low, wide = jnp.bfloat16, jnp.float32
    return pl.pallas_call(
        functools.partial(grads_kernel, sizes),
        out_shape=(
            jax.ShapeDtypeStruct((3, D, heads_dev), low),
            jax.ShapeDtypeStruct((heads_dev, D), low),
            jax.ShapeDtypeStruct((replicas - 1, 4, PAIR, D), low),
            jax.ShapeDtypeStruct((D // 128, 128), wide),
            jax.ShapeDtypeStruct((4, PART, D), low),
            jax.ShapeDtypeStruct((4, PART, D), low),
        ),
        in_specs=[vmem] * 7 + [hbm],
        out_specs=(hbm, hbm, hbm, vmem, vmem, vmem),
        scratch_shapes=[
            pltpu.VMEM((tokens, D // 2), low),
            pltpu.VMEM((tokens, D // 2), low),
            pltpu.VMEM((4, tokens, heads_dev), low),
            pltpu.VMEM((3, rows, heads_dev), low),
            pltpu.VMEM((heads_dev, rows), low),
            pltpu.VMEM((count - 1, 3, rows, heads_dev), low),
            pltpu.VMEM((count - 1, heads_dev, rows), low),
            pltpu.VMEM((3, rows, heads_dev), wide),
            pltpu.VMEM((heads_dev, rows), wide),
            pltpu.VMEM((friends + 1, D // 128, 128), wide),
            pltpu.VMEM((friends, D // 128, 128), wide),
            pltpu.VMEM((4, PAIR, D), low),
            pltpu.VMEM((4, PAIR, D), wide),
            pltpu.VMEM((4, PAIR, D), low),
            pltpu.VMEM((4, PAIR, D), low),
            dma((6,)),
            dma((6,)),
            dma((count - 1, 4)),
            dma((count - 1, 4)),
            dma((count - 1, 4)),
            dma((count - 1, 4)),
            dma((count, 4)),
            dma((count, 4)),
            dma((replicas - 1,)),
            dma((replicas - 1,)),
            dma((3,)),
            dma((3,)),
            dma((friends,)),
            dma((friends,)),
            dma((7,)),
        ],
        compiler_params=pltpu.CompilerParams(
            collective_id=2, has_side_effects=True, vmem_limit_bytes=60 * 1024 * 1024
        ),
    )(x, c, y, gain, token_blocks, grad_blocks, norm_gain, back)


def attention_kernel(
    group,
    blocked_ref,
    arrived_ref,
    w_ref,
    out_w_ref,
    gain_ref,
    y_ref,
    x_ref,
    c_ref,
    back_ref,
    gain_out,
    q_low,
    k_low,
    v_low,
    d_low,
    branch_acc,
    rolled_acc,
):
    step = pl.program_id(1)

    @pl.when(step == 0)
    def _():
        for window in range(group):
            parts = [arrived_ref[window, block].astype(jnp.float32) for block in range(4)]
            at = slice(window * TILE, (window + 1) * TILE)
            x_ref[at] = jnp.concatenate([part[:PART] for part in parts], 0).astype(jnp.bfloat16)
            c_ref[at] = jnp.concatenate([part[PART:] for part in parts], 0).astype(jnp.bfloat16)

    scale = HEAD ** (-0.5)
    width = w_ref.shape[2]
    x, c = x_ref[...], c_ref[...]
    for index, target in enumerate((q_low, k_low, v_low)):
        target[...] = jnp.dot(x, w_ref[index], preferred_element_type=jnp.float32).astype(
            jnp.bfloat16
        )
    d_low[...] = contract_cols(c, out_w_ref[...]).astype(jnp.bfloat16)
    lane = lax.broadcasted_iota(jnp.int32, (TILE, 128), 1)
    lower = lane < HEAD
    contract = (((0,), (0,)), ((), ()))
    for window in range(group):
        blocked = blocked_ref[window] < 0
        at = slice(window * TILE, (window + 1) * TILE)
        for pair in range(width // 128):
            cols = slice(pair * 128, (pair + 1) * 128)
            q, k, v, d = q_low[at, cols], k_low[at, cols], v_low[at, cols], d_low[at, cols]
            results = []
            for head in range(2):
                mine = lower if head == 0 else jnp.logical_not(lower)
                q_head = jnp.where(mine, q, jnp.zeros_like(q))
                d_head = jnp.where(mine, d, jnp.zeros_like(d))
                scores = jnp.where(blocked, -1e30, contract_cols(q_head, k) * scale)
                exponent = jnp.exp(scores - jnp.max(scores, -1, keepdims=True))
                weights = exponent / jnp.sum(exponent, -1, keepdims=True)
                weights_low = weights.astype(jnp.bfloat16)
                d_weights = contract_cols(d_head, v)
                row_dots = jnp.sum(weights * d_weights, -1, keepdims=True)
                d_scores = (weights * (d_weights - row_dots) * scale).astype(jnp.bfloat16)
                results.append(
                    (
                        jnp.dot(d_scores, k, preferred_element_type=jnp.float32),
                        lax.dot_general(
                            d_scores, q, contract, preferred_element_type=jnp.float32
                        ),
                        lax.dot_general(
                            weights_low, d, contract, preferred_element_type=jnp.float32
                        ),
                        jnp.dot(weights_low, v, preferred_element_type=jnp.float32),
                    )
                )
            for index in range(4):
                y_ref[index, at, cols] = jnp.where(
                    lower, results[0][index], results[1][index]
                ).astype(jnp.bfloat16)

    branch = jnp.dot(y_ref[3], out_w_ref[...], preferred_element_type=jnp.float32)
    rolled = contract_cols(y_ref[0], w_ref[0])
    rolled += contract_cols(y_ref[1], w_ref[1])
    rolled += contract_cols(y_ref[2], w_ref[2])

    @pl.when(step == 0)
    def _():
        branch_acc[...] = branch
        rolled_acc[...] = rolled

    @pl.when(step > 0)
    def _():
        branch_acc[...] += branch
        rolled_acc[...] += rolled

    @pl.when(step == pl.num_programs(1) - 1)
    def _():
        for window in range(group):
            for block in range(4):
                start = window * TILE + block * PART
                at = slice(start, start + PART)
                both = jnp.concatenate([branch_acc[at], rolled_acc[at]], axis=0)
                back_ref[window, block] = both.astype(jnp.bfloat16)
        low = rolled_acc[...].astype(jnp.bfloat16)
        product = low.astype(jnp.float32) * x_ref[...].astype(jnp.float32)
        gain_out[0] = jnp.sum(product, 0, keepdims=True) / gain_ref[...]


def attention(arrived, w_three, w_out, gain, blocked):
    replicas = arrived.shape[0]
    total = replicas * TILE
    heads_dev = w_three.shape[2]
    width = min(256, heads_dev)
    group = 2
    tile = group * TILE
    low, wide = jnp.bfloat16, jnp.float32
    return pl.pallas_call(
        functools.partial(attention_kernel, group),
        grid=(total // tile, heads_dev // width),
        in_specs=[
            pl.BlockSpec((group, TILE, TILE), lambda g, j: (g, 0, 0)),
            pl.BlockSpec((group, 4, PAIR, D), lambda g, j: (g, 0, 0, 0)),
            pl.BlockSpec((3, D, width), lambda g, j: (0, 0, j)),
            pl.BlockSpec((width, D), lambda g, j: (j, 0)),
            pl.BlockSpec((1, D), lambda g, j: (0, 0)),
        ],
        out_specs=(
            pl.BlockSpec((4, tile, width), lambda g, j: (0, g, j)),
            pl.BlockSpec((tile, D), lambda g, j: (g, 0)),
            pl.BlockSpec((tile, D), lambda g, j: (g, 0)),
            pl.BlockSpec((group, 4, PAIR, D), lambda g, j: (g, 0, 0, 0)),
            pl.BlockSpec((1, 1, D), lambda g, j: (g, 0, 0)),
        ),
        out_shape=(
            jax.ShapeDtypeStruct((4, total, heads_dev), low),
            jax.ShapeDtypeStruct((total, D), low),
            jax.ShapeDtypeStruct((total, D), low),
            jax.ShapeDtypeStruct((replicas, 4, PAIR, D), low),
            jax.ShapeDtypeStruct((total // tile, 1, D), wide),
        ),
        scratch_shapes=[pltpu.VMEM((tile, width), low)] * 4 + [pltpu.VMEM((tile, D), wide)] * 2,
        compiler_params=pltpu.CompilerParams(
            dimension_semantics=("arbitrary", "arbitrary"), vmem_limit_bytes=48 * 1024 * 1024
        ),
    )(blocked, arrived, w_three, w_out, gain)


def block_kernel(
    sizes,
    blocked_ref,
    token_ref,
    grad_ref,
    gain_ref,
    w_ref,
    out_w_ref,
    y_ref,
    x_ref,
    c_ref,
    back_ref,
    gain_out,
    src,
    arrived,
    q_low,
    k_low,
    v_low,
    d_low,
    att_low,
    weights_ref,
    branch_acc,
    rolled_acc,
    send_sem,
    recv_sem,
):
    group = sizes[0]
    step = pl.program_id(0)
    steps = pl.num_programs(0) // 2
    column = lax.rem(step, steps)
    scale = HEAD ** (-0.5)
    width = w_ref.shape[2]
    routes = gather_routes(sizes)
    routes = [r for r in routes if (r[0], r[1]) != (0, 0)]
    routes = [r for r in routes if r[0] > 0] + [r for r in routes if r[0] == 0]
    outer, _, _ = position()
    ranges = (pl.ds(0, 48), pl.ds(48, 32))

    def front_copy(index, part, tile):
        _, block, target, _, _, _ = routes[index]
        return pltpu.make_async_remote_copy(
            src.at[block, ranges[part]],
            arrived.at[tile, block, ranges[part]],
            send_sem.at[part, index],
            recv_sem.at[part, index],
            device_id=target,
            device_id_type=MESH,
        )

    @pl.when(step == 0)
    def _():
        for block in range(4):
            standard, _ = standardize(token_ref[block].astype(jnp.float32))
            both = [standard * gain_ref[...], grad_ref[block].astype(jnp.float32)]
            src[block] = jnp.concatenate(both, axis=0).astype(jnp.bfloat16)
        enter([r[2] for r in routes], [r[4] for r in routes])
        for index, route in enumerate(routes):
            front_copy(index, 0, route[3]).start()
        arrived[outer, 0] = src[0]
        for index, route in enumerate(routes):
            front_copy(index, 0, route[3]).wait_send()
        for index, route in enumerate(routes):
            front_copy(index, 1, route[3]).start()
        for index, route in enumerate(routes):
            front_copy(index, 0, route[5]).wait_recv()
        for window in range(group):
            parts = [arrived[window, b, :48].astype(jnp.float32)[:PART] for b in range(4)]
            at = slice(window * TILE, (window + 1) * TILE)
            x_ref[at] = jnp.concatenate(parts, 0).astype(jnp.bfloat16)

    @pl.when(step == steps)
    def _():
        for index, route in enumerate(routes):
            front_copy(index, 1, route[5]).wait_recv()
        for index, route in enumerate(routes):
            front_copy(index, 1, route[3]).wait_send()
        for window in range(group):
            parts = [arrived[window, b].astype(jnp.float32)[PART:] for b in range(4)]
            at = slice(window * TILE, (window + 1) * TILE)
            c_ref[at] = jnp.concatenate(parts, 0).astype(jnp.bfloat16)

    lower = lax.broadcasted_iota(jnp.int32, (TILE, 128), 1) < HEAD
    contract = (((0,), (0,)), ((), ()))
    units = [(window, pair) for window in range(group) for pair in range(width // 128)]

    def region(window, pair):
        return (
            slice(window * TILE, (window + 1) * TILE),
            slice(pair * 128, (pair + 1) * 128),
        )

    @pl.when(step < steps)
    def _():
        x = x_ref[...]
        for index, target in enumerate((q_low, k_low, v_low)):
            target[column] = jnp.dot(
                x, w_ref[index], preferred_element_type=jnp.float32
            ).astype(jnp.bfloat16)
        for unit, (window, pair) in enumerate(units):
            blocked = blocked_ref[window] < 0
            at, cols = region(window, pair)
            q, k, v = q_low[column, at, cols], k_low[column, at, cols], v_low[column, at, cols]
            results = []
            for head in range(2):
                mine = lower if head == 0 else jnp.logical_not(lower)
                q_head = jnp.where(mine, q, jnp.zeros_like(q))
                scores = jnp.where(blocked, -1e30, contract_cols(q_head, k) * scale)
                exponent = jnp.exp(scores - jnp.max(scores, -1, keepdims=True))
                weights = exponent / jnp.sum(exponent, -1, keepdims=True)
                weights_ref[column, 2 * unit + head] = weights
                results.append(
                    jnp.dot(weights.astype(jnp.bfloat16), v, preferred_element_type=jnp.float32)
                )
            att_low[column, at, cols] = jnp.where(lower, results[0], results[1]).astype(
                jnp.bfloat16
            )

    @pl.when(step >= steps)
    def _():
        d_low[...] = contract_cols(c_ref[...], out_w_ref[...]).astype(jnp.bfloat16)
        for unit, (window, pair) in enumerate(units):
            at, cols = region(window, pair)
            q, k, v = q_low[column, at, cols], k_low[column, at, cols], v_low[column, at, cols]
            d = d_low[at, cols]
            results = []
            for head in range(2):
                mine = lower if head == 0 else jnp.logical_not(lower)
                d_head = jnp.where(mine, d, jnp.zeros_like(d))
                weights = weights_ref[column, 2 * unit + head]
                weights_low = weights.astype(jnp.bfloat16)
                d_weights = contract_cols(d_head, v)
                row_dots = jnp.sum(weights * d_weights, -1, keepdims=True)
                d_scores = (weights * (d_weights - row_dots) * scale).astype(jnp.bfloat16)
                results.append(
                    (
                        jnp.dot(d_scores, k, preferred_element_type=jnp.float32),
                        lax.dot_general(
                            d_scores, q, contract, preferred_element_type=jnp.float32
                        ),
                        lax.dot_general(
                            weights_low, d, contract, preferred_element_type=jnp.float32
                        ),
                    )
                )
            for index in range(3):
                y_ref[index, at, cols] = jnp.where(
                    lower, results[0][index], results[1][index]
                ).astype(jnp.bfloat16)
        y_ref[3] = att_low[column]
        branch = jnp.dot(y_ref[3], out_w_ref[...], preferred_element_type=jnp.float32)
        rolled = contract_cols(y_ref[0], w_ref[0])
        rolled += contract_cols(y_ref[1], w_ref[1])
        rolled += contract_cols(y_ref[2], w_ref[2])

        @pl.when(step == steps)
        def _():
            branch_acc[...] = branch
            rolled_acc[...] = rolled

        @pl.when(step > steps)
        def _():
            branch_acc[...] += branch
            rolled_acc[...] += rolled

    @pl.when(step == 2 * steps - 1)
    def _():
        for window in range(group):
            for block in range(4):
                start = window * TILE + block * PART
                at = slice(start, start + PART)
                both = jnp.concatenate([branch_acc[at], rolled_acc[at]], axis=0)
                back_ref[window, block] = both.astype(jnp.bfloat16)
        low = rolled_acc[...].astype(jnp.bfloat16)
        product = low.astype(jnp.float32) * x_ref[...].astype(jnp.float32)
        gain_out[0] = jnp.sum(product, 0, keepdims=True) / gain_ref[...]


def front_and_attention(sizes, token_blocks, grad_blocks, w_three, w_out, gain, blocked):
    replicas = sizes[0]
    total = replicas * TILE
    heads_dev = w_three.shape[2]
    width = min(256, heads_dev)
    steps = heads_dev // width
    count = 4 * replicas - 1
    low, wide = jnp.bfloat16, jnp.float32

    def later(i):
        return jnp.maximum(i - steps, 0)

    def whole(*shape):
        return pl.BlockSpec(shape, lambda i: (0,) * len(shape))

    return pl.pallas_call(
        functools.partial(block_kernel, sizes),
        grid=(2 * steps,),
        in_specs=[
            whole(replicas, TILE, TILE),
            whole(4, PART, D),
            whole(4, PART, D),
            whole(1, D),
            pl.BlockSpec((3, D, width), lambda i: (0, 0, lax.rem(i, steps))),
            pl.BlockSpec((width, D), lambda i: (later(i), 0)),
        ],
        out_specs=(
            pl.BlockSpec((4, total, width), lambda i: (0, 0, later(i))),
            whole(total, D),
            whole(total, D),
            whole(replicas, 4, PAIR, D),
            whole(1, 1, D),
        ),
        out_shape=(
            jax.ShapeDtypeStruct((4, total, heads_dev), low),
            jax.ShapeDtypeStruct((total, D), low),
            jax.ShapeDtypeStruct((total, D), low),
            jax.ShapeDtypeStruct((replicas, 4, PAIR, D), low),
            jax.ShapeDtypeStruct((1, 1, D), wide),
        ),
        scratch_shapes=[
            pltpu.VMEM((4, PAIR, D), low),
            pltpu.VMEM((replicas, 4, PAIR, D), low),
            pltpu.VMEM((steps, total, width), low),
            pltpu.VMEM((steps, total, width), low),
            pltpu.VMEM((steps, total, width), low),
            pltpu.VMEM((total, width), low),
            pltpu.VMEM((steps, total, width), low),
            pltpu.VMEM((steps, replicas * width // HEAD, TILE, TILE), wide),
            pltpu.VMEM((total, D), wide),
            pltpu.VMEM((total, D), wide),
            pltpu.SemaphoreType.DMA((2, count)),
            pltpu.SemaphoreType.DMA((2, count)),
        ],
        compiler_params=pltpu.CompilerParams(
            collective_id=3,
            has_side_effects=True,
            dimension_semantics=("arbitrary",),
            vmem_limit_bytes=56 * 1024 * 1024,
        ),
    )(blocked, token_blocks, grad_blocks, gain, w_three, w_out)


def contract_cols(left, right):
    return lax.dot_general(
        left, right, (((1,), (1,)), ((), ())), preferred_element_type=jnp.float32
    )


def to_blocks(tensor):
    shaped = tensor.reshape(2, CLAT, 2, WLON // 2, LEV, D)
    blocks = [shaped[1 - a, :, 1 - b].reshape(QUARTER, D) for a in range(2) for b in range(2)]
    return jnp.pad(jnp.stack(blocks), ((0, 0), (0, PART - QUARTER), (0, 0)))


def from_blocks(blocks):
    shaped = blocks[:, :QUARTER].reshape(2, 2, CLAT, WLON // 2, LEV, D)
    rows = [jnp.concatenate([shaped[a, 1], shaped[a, 0]], axis=1) for a in (1, 0)]
    return jnp.concatenate(rows, axis=0)


def shards(tokens, norm_gain, w_qkv, w_out, grad_out):
    sizes = tuple(lax.axis_size(name) for name in ("outer", "lat", "lon"))
    replicas, lat_count, lon_count = sizes
    assert tokens.shape[:3] == (2 * CLAT, LEV, WLON)
    lat_index = lax.axis_index("lat")
    w_three = w_qkv.transpose(1, 0, 2)
    gain = norm_gain.reshape(1, D)
    token_blocks = to_blocks(tokens.transpose(0, 2, 1, 3))
    grad_blocks = to_blocks(grad_out.transpose(0, 2, 1, 3))
    cut_window = jnp.logical_and(lat_index == lat_count - 1, jnp.arange(replicas) == replicas - 1)
    spot = jnp.arange(TILE)
    half_index = spot // (2 * PART)
    other_half = half_index[:, None] != half_index[None, :]
    blocked = jnp.logical_and(cut_window[:, None, None], other_half[None])
    blocked = jnp.logical_or(blocked, (spot % PART >= QUARTER)[None, None])
    blocked = jnp.where(blocked, -1.0, 0.0).astype(jnp.float32)
    if replicas == 2:
        y, x, c, back, gain_local = front_and_attention(
            sizes, token_blocks, grad_blocks, w_three, w_out, gain, blocked
        )
    else:
        arrived = front_exchange(sizes, token_blocks, grad_blocks, gain)
        y, x, c, back, gain_local = attention(arrived, w_three, w_out, gain, blocked)
    gain_local = jnp.sum(gain_local, (0, 1)).reshape(D // 128, 128)
    grad_qkv, grad_out_w, _, grad_gain, output, grad_tokens = grads_exchange(
        sizes, x, c, y, gain_local, token_blocks, grad_blocks, gain, back
    )
    grad_wqkv = grad_qkv.astype(jnp.float32).transpose(1, 0, 2)
    grad_wout = grad_out_w.astype(jnp.float32)
    return (
        from_blocks(output).transpose(0, 2, 1, 3),
        from_blocks(grad_tokens).transpose(0, 2, 1, 3),
        grad_wqkv,
        grad_wout,
        grad_gain.reshape(D),
    )


def solution(mesh):
    in_specs = (
        P(("outer", "lat"), None, "lon", None),
        P(),
        P(None, None, "outer"),
        P("outer", None),
        P(("outer", "lat"), None, "lon", None),
    )
    out_specs = (
        P(("outer", "lat"), None, "lon", None),
        P(("outer", "lat"), None, "lon", None),
        P(None, None, "outer"),
        P("outer", None),
        P(),
    )
    return jax.shard_map(shards, mesh=mesh, in_specs=in_specs, out_specs=out_specs, check_vma=False)
```
